32 devices in a mesh: wide: 4 (over x, core), narrow: 8 (over z, y).
Axes of the slice: x: 2, y: 2, z: 4, core: 2. Of those that a mesh axis runs over, the one named last changes fastest.
Arguments:
- right_side: float32 [512, 128, 128], P(('wide', 'narrow')), may hold values from -120 to 120
- resistance: float32 [512, 128], P(('wide', 'narrow')), may hold values from 0.3 to 3
- omega: float32 [32], replicated, may hold values from 0.5 to 2
- pcoef: float32 [32768], P(('wide', 'narrow')), may hold values from 0.1 to 1
- branch_nodes: int32 [512, 2, 128], P(('wide', 'narrow')), may hold values from 0 to 2047, as said below
- self_blocks: bfloat16 [512, 128, 128], P(('wide', 'narrow')), may hold values from -1 to 3
- couple_list: int32 [3, 7168], P(None, ('wide', 'narrow')), may hold values from 0 to 15, as said below
- couple_blocks: bfloat16 [7168, 128, 128], P(('wide', 'narrow')), may hold values from -0.109375 to 0.109375
- jacobi_ids: int32 [512], P(('wide', 'narrow')), may hold values from 0 to 7
- preconditioners: bfloat16 [8, 128, 128], replicated, may hold values from -1 to 2
Outputs:
- solution: float32 [512, 128, 128], P(('wide', 'narrow'))
- residual_norms: float32 [2, 32], replicated
The draws below stay inside these ranges and needn't reach their ends.
Inputs may be any that keep to these rules, and one draw needn't show every extreme that they name: `couple_list`: row 0 names a row block of the entry's device, row 1 a block of the owner, row 2 the owner's narrow index in the same wide group. Over the entries of one device, at most 4 distinct blocks of one owner are named; exactly 4 of the device itself, and at least one of every owner. No pair of row block and source block appears twice. `branch_nodes`: A value v of 1024 or more names node v - 1024 of the next device along narrow in the same wide group; such values never stand on the last device along narrow.
All inputs are finite; a program needn't handle non-finite values.
Results may differ from the reference program's by a relative error of at most 0.0034.
Values may be sent and summed in bfloat16 or wider, within the bound.
No kernel may reach another device: no remote copies, remote signals or barrier semaphores. Data moves between devices by JAX's collectives and lax.ppermute only.
A program may use at most 128 MiB of HBM per device.

```python
import math
import jax
import jax.numpy as jnp
from jax import lax

B = 128
F = 32
CASES = 2
NB_DEV = 16
CAP = 4
ITERS = 3
NJ = 8
PEERS = 8
C = 128
E_DEV = 224
NODE_DEV = 1024
NBLK = 512
TOTAL_E = 7168
NODES = 32768


def draw_right_side(key, part):
    ramp = 1.0 + 0.732 * jnp.arange(NBLK, dtype=jnp.float32) / max(NBLK - 1, 1)
    row_scale = jnp.exp(jax.random.uniform(jax.random.fold_in(key, 1), (NBLK, B, 1), jnp.float32, math.log(0.3), math.log(3.0)))
    column_scale = jnp.exp(jax.random.uniform(jax.random.fold_in(key, 2), (1, 1, C), jnp.float32, math.log(0.5), math.log(5.0)))
    values = jnp.clip(jax.random.normal(jax.random.fold_in(key, 3), (NBLK, B, C), jnp.float32), -4.0, 4.0)
    return values * row_scale * column_scale * ramp[:, None, None]


def draw_self_blocks(key, part):
    identity = jnp.eye(B, dtype=jnp.float32)
    diagonal = jax.random.uniform(jax.random.fold_in(key, 1), (NBLK, B, 1), jnp.float32, 1.0, 2.0)
    spread = jnp.clip(jax.random.normal(jax.random.fold_in(key, 2), (NBLK, B, B), jnp.float32), -4.0, 4.0)
    return (identity * diagonal + spread * (0.5 / math.sqrt(B))).astype(jnp.bfloat16)


def draw_preconditioners(key, part):
    identity = jnp.eye(B, dtype=jnp.float32)
    diagonal = jax.random.uniform(jax.random.fold_in(key, 1), (NJ, B, 1), jnp.float32, 0.5, 1.5)
    spread = jnp.clip(jax.random.normal(jax.random.fold_in(key, 2), (NJ, B, B), jnp.float32), -4.0, 4.0)
    return (identity * diagonal + spread * (0.3 / math.sqrt(B))).astype(jnp.bfloat16)


def draw_branch_nodes(key, part):
    blocks = jnp.arange(NBLK, dtype=jnp.int32)
    last_peer = blocks // NB_DEV % PEERS == PEERS - 1
    node = jax.random.randint(jax.random.fold_in(key, 1), (NBLK, 2, B), 0, NODE_DEV)
    side = jax.random.randint(jax.random.fold_in(key, 2), (NBLK, 2, B), 0, 4)
    beyond = (side == 0) & jnp.logical_not(last_peer)[:, None, None]
    return jnp.where(beyond, node + NODE_DEV, node).astype(jnp.int32)


def draw_couple_list(key, part):
    devices = NBLK // NB_DEV
    device = jnp.arange(devices, dtype=jnp.int32)
    mine = device % PEERS
    owners = jnp.arange(PEERS, dtype=jnp.int32)
    distance = jnp.abs(owners[None, :] - mine[:, None])
    counts = jnp.maximum(1, CAP // jnp.maximum(distance, 1))
    ends = jnp.cumsum(counts, axis=1)
    starts = ends - counts
    total = ends[:, -1:]
    entry = jnp.arange(E_DEV, dtype=jnp.int32)
    pick = entry[None, :] % total
    lap = entry[None, :] // total
    shifts = jax.random.randint(jax.random.fold_in(key, 1), (devices, E_DEV), 0, NB_DEV)
    shift = jnp.take_along_axis(shifts, pick, axis=1)
    row = (lap + shift) % NB_DEV
    owner = jnp.sum((ends[:, None, :] <= pick[:, :, None]).astype(jnp.int32), axis=2)
    within = pick - jnp.take_along_axis(starts, owner, axis=1)
    scores = jax.random.randint(jax.random.fold_in(key, 2), (devices, PEERS, NB_DEV), 0, 1 << 20) * NB_DEV + jnp.arange(NB_DEV, dtype=jnp.int32)
    order = jnp.argsort(scores, axis=2)
    column = order[device[:, None], owner, within]
    return jnp.stack([row.reshape(-1), column.reshape(-1), owner.reshape(-1)]).astype(jnp.int32)


def place_ends(values, rng, smallest, top_value):
    dims = values.shape
    place = [jax.random.randint(jax.random.fold_in(rng, axis), (), 0, dims[axis]) for axis in range(len(dims))]
    values = values.at[tuple(place)].set(smallest)
    longest = dims.index(max(dims))
    place[longest] = (place[longest] + 1) % dims[longest]
    return values.at[tuple(place)].set(top_value)


def block_levels(stream_key, dims, cuts, least, top_value):
    factor_of = 1.0
    for dim, blocks in cuts:
        draws = jax.random.uniform(jax.random.fold_in(jax.random.fold_in(stream_key, 6), dim), (blocks,), jnp.float32, least / len(cuts), top_value / len(cuts))
        factor_of = factor_of * jnp.repeat(jnp.exp(draws), dims[dim] // blocks).reshape((-1,) + (1,) * (len(dims) - 1 - dim))
    return factor_of


def normal_values(rng, shape, deviation, limit, split=(), kind=jnp.bfloat16):
    values = jax.random.normal(rng, shape, jnp.float32) * deviation
    if len(split) > 0:
        values = block_levels(rng, shape, split, -0.22, 0.18) * values
    return jnp.clip(values, min=-limit, max=limit).astype(kind)


def setup_inputs(seed: int = 0) -> dict:
    key_list = jax.random.split(jax.random.key(seed), 11)
    return {
        "right_side": draw_right_side(jax.random.fold_in(key_list[10], 71), 0),
        "resistance": jnp.clip(jnp.exp(math.log(3.0) - 2.3025851 * jax.random.uniform(key_list[1], (NBLK, B), jnp.float32) ** block_levels(key_list[1], (NBLK, B), ((0, 32),), -0.2, 0.2)), 0.3, 3.0),
        "omega": jnp.clip(jnp.exp(jax.random.uniform(key_list[2], (F,), jnp.float32, math.log(0.5), math.log(2.0))), 0.5, 2.0),
        "pcoef": jnp.clip(jnp.exp(math.log(1.0) - 2.3025851 * jax.random.uniform(key_list[3], (NODES,), jnp.float32) ** block_levels(key_list[3], (NODES,), ((0, 32),), -0.2, 0.2)), 0.1, 1.0),
        "branch_nodes": draw_branch_nodes(jax.random.fold_in(key_list[10], 71), 0),
        "self_blocks": draw_self_blocks(jax.random.fold_in(key_list[10], 71), 0),
        "couple_list": draw_couple_list(jax.random.fold_in(key_list[10], 71), 0),
        "couple_blocks": normal_values(key_list[7], (TOTAL_E, B, B), (22 * B) ** -0.5, 0.109375, ((0, 32),)),
        "jacobi_ids": place_ends(jax.random.randint(key_list[8], (NBLK,), 0, NJ), jax.random.fold_in(key_list[8], 1), 0, NJ - 1).astype(jnp.int32),
        "preconditioners": draw_preconditioners(jax.random.fold_in(key_list[10], 71), 0),
    }


def system_dot(first, second):
    return lax.optimization_barrier(jnp.sum((first * second).reshape(-1, CASES, 2, F), axis=(0, 2)))

def expand(values):
    return jnp.broadcast_to(values[:, None, :], (CASES, 2, F)).reshape(2 * CASES * F)

def turned(values):
    parts = values.reshape(values.shape[:-1] + (CASES, 2, F))
    return jnp.stack([-parts[..., 1, :], parts[..., 0, :]], axis=-2).reshape(values.shape)

def inductive(rounded, self_blocks, couple_list, couple_blocks):
    devices = NBLK // NB_DEV
    own = jnp.einsum('nab,nbc->nac', self_blocks.astype(jnp.float32), rounded.astype(jnp.float32))
    rows = couple_list[0].reshape(devices, E_DEV)
    cols = couple_list[1].reshape(devices, E_DEV)
    owners = couple_list[2].reshape(devices, E_DEV)
    blocks = couple_blocks.reshape(devices, E_DEV, B, B)

    def one_device(items):
        device, row, col, owner, block = items
        group = device // PEERS
        source = ((group * PEERS + owner) * NB_DEV + col).astype(jnp.int32)
        gathered = jnp.take(rounded, source, axis=0).astype(jnp.float32)
        product = jnp.einsum('eab,ebc->eac', block.astype(jnp.float32), gathered)
        return jax.ops.segment_sum(product, row, NB_DEV)
    coupled = lax.map(one_device, (jnp.arange(devices, dtype=jnp.int32), rows, cols, owners, blocks))
    return own + coupled.reshape(NBLK, B, 2 * CASES * F)

def node_drop(field, branch_nodes, pcoef):
    device = jnp.arange(NBLK, dtype=jnp.int32) // NB_DEV
    glob = branch_nodes + (device * NODE_DEV)[:, None, None]
    rows = field.reshape(NBLK * B, 2 * CASES * F)
    first = glob[:, 0, :].reshape(-1)
    second = glob[:, 1, :].reshape(-1)
    charge = jax.ops.segment_sum(rows, first, NODES) - jax.ops.segment_sum(rows, second, NODES)
    potential = pcoef[:, None] * charge
    drop = jnp.take(potential, first, axis=0) - jnp.take(potential, second, axis=0)
    return drop.reshape(NBLK, B, 2 * CASES * F)

def least_squares(hess, beta):
    zero = jnp.zeros_like(beta)
    rotated = [beta] + [zero for later in range(ITERS)]
    cosines = []
    sines = []
    upper = [[None for later in range(ITERS)] for other in range(ITERS)]
    for column in range(ITERS):
        entries = [hess[index][column] for index in range(column + 1)] + [hess[column + 1][column]]
        for index in range(column):
            top = entries[index]
            low = entries[index + 1]
            entries[index] = cosines[index] * top + sines[index] * low
            entries[index + 1] = -sines[index] * top + cosines[index] * low
        top = entries[column]
        low = entries[column + 1]
        radius = jnp.sqrt(top * top + low * low)
        cosine = top / radius
        sine = low / radius
        cosines.append(cosine)
        sines.append(sine)
        entries[column] = radius
        rotated[column + 1] = -sine * rotated[column]
        rotated[column] = cosine * rotated[column]
        for index in range(column + 1):
            upper[index][column] = entries[index]
    weights = [None for later in range(ITERS)]
    for index in reversed(range(ITERS)):
        accum = rotated[index]
        for other in range(index + 1, ITERS):
            accum = accum - upper[index][other] * weights[other]
        weights[index] = accum / upper[index][index]
    return (weights, jnp.abs(rotated[ITERS]))

def reference(right_side, resistance, omega, pcoef, branch_nodes, self_blocks, couple_list, couple_blocks, jacobi_ids, preconditioners):
    frequency = jnp.tile(omega, 2 * CASES)
    chosen = jnp.take(preconditioners, jacobi_ids, axis=0).astype(jnp.float32)

    def operate(field):
        rounded = field.astype(jnp.bfloat16)
        flux = inductive(rounded, self_blocks, couple_list, couple_blocks)
        drop = node_drop(field, branch_nodes, pcoef)
        return resistance[:, :, None] * field + turned(frequency * flux - drop / frequency)
    beta = jnp.sqrt(system_dot(right_side, right_side))
    basis = [right_side / expand(beta)]
    directions = []
    hess = [[None for later in range(ITERS)] for other in range(ITERS + 1)]
    for column in range(ITERS):
        direction = jnp.einsum('nab,nbc->nac', chosen, basis[column].astype(jnp.bfloat16).astype(jnp.float32))
        directions.append(direction)
        image = operate(direction)
        projected = [system_dot(basis[index], image) for index in range(column + 1)]
        for index in range(column + 1):
            image = image - expand(projected[index]) * basis[index]
            hess[index][column] = projected[index]
        length = jnp.sqrt(system_dot(image, image))
        hess[column + 1][column] = length
        if column + 1 < ITERS:
            basis.append(image / expand(length))
    weights, residual_norms = least_squares(hess, beta)
    solution = expand(weights[0]) * directions[0]
    for column in range(1, ITERS):
        solution = solution + expand(weights[column]) * directions[column]
    return (solution, residual_norms)
```

```python
import functools
import jax
import jax.numpy as jnp
from jax import lax
from jax.experimental import pallas as pl
from jax.experimental.pallas import tpu as pltpu
from jax.sharding import PartitionSpec as P

F = 32
CASES = 2
ITERS = 3
CAP = 4
AXES = ("wide", "narrow")
STEP = 2.0**-8
LIMIT = 60 * 1024 * 1024
f32 = jnp.float32
bf16 = jnp.bfloat16
i32 = jnp.int32


def whole(shape, dtype):
    return jax.ShapeDtypeStruct(shape, dtype)


VM = pl.BlockSpec(memory_space=pltpu.VMEM)
SM = pl.BlockSpec(memory_space=pltpu.SMEM)


def lane_is_real(shape):
    lane = lax.broadcasted_iota(i32, shape, len(shape) - 1)
    return lax.rem(lane, 2 * F) < F


def both_parts(row):
    other = jnp.where(lane_is_real(row.shape), pltpu.roll(row, 128 - F, 1), pltpu.roll(row, F, 1))
    return row + other


def turned(values):
    return jnp.where(
        lane_is_real(values.shape),
        -pltpu.roll(values, 128 - F, 1),
        pltpu.roll(values, F, 1),
    )


def setup_kernel(peers, blocks, lists_ref, right_ref, pcoef_ref, pay_ref, slot_ref):
    keys = peers * blocks
    entries = lists_ref.shape[1]
    column = lists_ref[1:2, :]
    owner = lists_ref[2:3, :]
    key = owner * blocks + column
    one = (lax.broadcasted_iota(i32, (keys, entries), 0) == key).astype(f32)
    present = jnp.max(one, axis=1, keepdims=True)
    row = lax.broadcasted_iota(i32, (keys, keys), 0)
    col = lax.broadcasted_iota(i32, (keys, keys), 1)
    before = jnp.where((row // blocks == col // blocks) & (col <= row), 1.0, 0.0).astype(bf16)
    rank = jnp.dot(
        before,
        jnp.broadcast_to(present, (keys, 128)).astype(bf16),
        preferred_element_type=f32,
    )
    place = jnp.sum(one * (rank[:, :1] - 1.0), axis=0, keepdims=True)
    slot_ref[...] = owner * CAP + place.astype(i32)
    lane = lax.broadcasted_iota(i32, (keys, 128), 1)
    name = lax.broadcasted_iota(i32, (keys, 128), 0)
    chosen = (
        (name // blocks == lane // CAP)
        & (rank == (lane % CAP + 1).astype(f32))
        & (present > 0.0)
    )
    needs = jnp.sum(jnp.where(chosen, (name % blocks).astype(f32), 0.0), axis=0, keepdims=True)
    right = right_ref[...]
    squares = jnp.sum(jnp.sum(right * right, axis=0), axis=0, keepdims=True)
    rows = jnp.concatenate([squares, needs, jnp.zeros((6, 128), f32), pcoef_ref[...]], axis=0)
    pay_ref[...] = jnp.broadcast_to(rows[None], pay_ref.shape)


def emit(w_of, jacobi_ref, needs_ref, table_ref, ends_ref, z_ref, zb_ref, send_ref, near_ref, far_ref):
    blocks = z_ref.shape[0]
    size = z_ref.shape[1]
    nodes = near_ref.shape[0]
    for n in range(blocks):
        z = jnp.dot(table_ref[jacobi_ref[n]], w_of(n).astype(bf16), preferred_element_type=f32)
        z_ref[n] = z
        zb_ref[n] = z.astype(bf16)
    peers = send_ref.shape[0]
    for j in range(peers):
        for s in range(CAP):
            send_ref[j, s] = zb_ref[needs_ref[j, s]]
    field = zb_ref[...].reshape(blocks * size, zb_ref.shape[2])
    chunk = 256
    for part, out in ((0, near_ref), (1, far_ref)):

        def body(step, carry, part=part, out=out):
            start = pl.multiple_of(step * chunk, chunk)
            node = lax.broadcasted_iota(i32, (chunk, blocks * size), 0) + (start + part * nodes)
            first = (node == ends_ref[0:1, :]).astype(f32)
            second = (node == ends_ref[1:2, :]).astype(f32)
            gather = (first - second).astype(bf16)
            out[pl.ds(start, chunk), :] = jnp.dot(
                gather, field, preferred_element_type=f32
            ).astype(bf16)
            return carry

        lax.fori_loop(0, nodes // chunk, body, 0)


def start_kernel(
    pay_ref, right_ref, jacobi_ref, needs_ref, table_ref, ends_ref,
    w_ref, z_ref, zb_ref, send_ref, near_ref, far_ref, beta_ref,
):
    total = jnp.sum(pay_ref[:, 0, :], axis=0, keepdims=True)
    beta = jnp.sqrt(both_parts(total))
    beta_ref[...] = jnp.broadcast_to(beta, beta_ref.shape)
    w_ref[...] = right_ref[...] / beta[None]
    emit(
        lambda n: w_ref[n], jacobi_ref, needs_ref, table_ref, ends_ref,
        z_ref, zb_ref, send_ref, near_ref, far_ref,
    )


def local_kernel(
    z_ref, zb_ref, self_ref, res_ref, freq_ref, near_ref, far_ref, arrived_ref, beyond_ref,
    scale_ref, cols_ref, part_ref, pot_ref,
):
    blocks, size, width = z_ref.shape
    nodes = near_ref.shape[0]
    pot_ref[:nodes] = (
        scale_ref[:nodes] * (near_ref[...].astype(f32) + arrived_ref[...].astype(f32))
    ).astype(bf16)
    pot_ref[nodes:] = (
        scale_ref[nodes:] * (far_ref[...].astype(f32) + beyond_ref[...].astype(f32))
    ).astype(bf16)
    freq = freq_ref[...]

    def body(n, carry):
        start = pl.multiple_of(n * size, size)
        ends = cols_ref[pl.ds(start, size), :]
        node = lax.broadcasted_iota(i32, (size, 2 * nodes), 1)
        first = (node == ends[:, 0:1]).astype(f32)
        second = (node == ends[:, 1:2]).astype(f32)
        spread = (first - second).astype(bf16)
        drop = jnp.dot(spread, pot_ref[...], preferred_element_type=f32)
        flux = jnp.dot(self_ref[n], zb_ref[n], preferred_element_type=f32)
        part_ref[n] = res_ref[pl.ds(start, size), :] * z_ref[n] + turned(freq * flux - drop / freq)
        return carry

    lax.fori_loop(0, blocks, body, 0)


def couple_step(entries, row_ref, slot_ref, couple_ref, arrived_ref, acc_ref):
    step = pl.program_id(0)

    @pl.when(step == 0)
    def _():
        acc_ref[...] = jnp.zeros_like(acc_ref)

    for j in range(entries):
        e = step * entries + j
        row = row_ref[e]
        acc_ref[row] += jnp.dot(
            couple_ref[j], arrived_ref[slot_ref[e]], preferred_element_type=f32
        )


def image_of(part_ref, freq_ref, acc_ref, n):
    return STEP * (part_ref[n] + turned(freq_ref[...] * acc_ref[n]))


def middle_kernel(
    entries, row_ref, slot_ref, couple_ref, arrived_ref, part_ref, freq_ref,
    jacobi_ref, needs_ref, table_ref, ends_ref,
    w_ref, z_ref, zb_ref, send_ref, near_ref, far_ref, acc_ref,
):
    couple_step(entries, row_ref, slot_ref, couple_ref, arrived_ref, acc_ref)

    @pl.when(pl.program_id(0) == pl.num_programs(0) - 1)
    def _():
        for n in range(w_ref.shape[0]):
            w_ref[n] = image_of(part_ref, freq_ref, acc_ref, n)
        emit(
            lambda n: w_ref[n], jacobi_ref, needs_ref, table_ref, ends_ref,
            z_ref, zb_ref, send_ref, near_ref, far_ref,
        )


PAIRS = [(i, j) for j in range(ITERS + 1) for i in range(j + 1)]


def last_kernel(
    entries, row_ref, slot_ref, couple_ref, arrived_ref, part_ref, freq_ref,
    w0_ref, w1_ref, w2_ref, pay_ref, acc_ref,
):
    couple_step(entries, row_ref, slot_ref, couple_ref, arrived_ref, acc_ref)

    @pl.when(pl.program_id(0) == pl.num_programs(0) - 1)
    def _():
        blocks = acc_ref.shape[0]

        def body(n, sums):
            w = [w0_ref[n], w1_ref[n], w2_ref[n], image_of(part_ref, freq_ref, acc_ref, n)]
            fresh = []
            for at, (i, j) in enumerate(PAIRS):
                product = (w[i] * w[j]).reshape(-1, 8, 128)
                fresh.append(sums[at] + jnp.sum(product, axis=0))
            return tuple(fresh)

        sums = lax.fori_loop(0, blocks, body, tuple(jnp.zeros((8, 128), f32) for _ in PAIRS))
        rows = [jnp.sum(s, axis=0, keepdims=True) for s in sums]
        rows.append(jnp.zeros((16 - len(rows), 128), f32))
        pay_ref[...] = jnp.broadcast_to(jnp.concatenate(rows, axis=0)[None], pay_ref.shape)


def finish_kernel(pay_ref, beta_ref, z0_ref, z1_ref, z2_ref, out_ref, norm_ref):
    total = both_parts(jnp.sum(pay_ref[...], axis=0))
    gram = {}
    for at, (i, j) in enumerate(PAIRS):
        gram[i, j] = gram[j, i] = total[at : at + 1, :]
    order = list(range(1, ITERS + 1)) + [0]
    low = {}
    for i in range(ITERS + 1):
        for j in range(i + 1):
            value = gram[order[i], order[j]]
            for k in range(j):
                value = value - low[i, k] * low[j, k]
            low[i, j] = jnp.sqrt(jnp.maximum(value, 0.0)) if i == j else value / low[j, j]
    weights = [None] * ITERS
    for i in reversed(range(ITERS)):
        value = low[ITERS, i]
        for k in range(i + 1, ITERS):
            value = value - low[k, i] * weights[k]
        weights[i] = value / low[i, i]
    beta = beta_ref[0:1, :]
    norm_ref[...] = jnp.broadcast_to(low[ITERS, ITERS] * beta, norm_ref.shape)
    weights = [STEP * beta * weight for weight in weights]
    for n in range(out_ref.shape[0]):
        out_ref[n] = weights[0] * z0_ref[n] + weights[1] * z1_ref[n] + weights[2] * z2_ref[n]


def call(kernel, outs, ins, **more):
    return pl.pallas_call(
        kernel,
        out_shape=outs,
        in_specs=ins,
        out_specs=[VM] * len(outs),
        compiler_params=pltpu.CompilerParams(vmem_limit_bytes=LIMIT),
        **more,
    )


def on_device(
    right_side, resistance, omega, pcoef, branch_nodes, self_blocks, couple_list, couple_blocks,
    jacobi_ids, preconditioners,
):
    blocks, size, width = right_side.shape
    nodes = pcoef.shape[0]
    entries = couple_list.shape[1]
    peers = lax.axis_size("narrow")
    devices = peers * lax.axis_size("wide")
    group = lax.axis_index("wide")
    mine = lax.axis_index("narrow")
    node_rows = nodes // 128
    freq = jnp.tile(omega, 2 * CASES).reshape(1, width)
    ends = jnp.transpose(branch_nodes, (1, 0, 2)).reshape(2, blocks * size)
    ends_col = jnp.transpose(ends)
    res_col = resistance.reshape(blocks * size, 1)

    pay, slots = call(
        functools.partial(setup_kernel, peers, blocks),
        [whole((devices, 8 + node_rows, 128), f32), whole((1, entries), i32)],
        [VM] * 3,
    )(couple_list, right_side, pcoef.reshape(node_rows, 128))
    pay = lax.all_to_all(pay, AXES, 0, 0)
    slots = slots.reshape(entries)
    rows = couple_list[0]
    needs = lax.dynamic_slice(
        pay, (group * peers, 1, mine * CAP), (peers, 1, CAP)
    ).reshape(peers, CAP).astype(i32)
    next_dev = jnp.minimum(group * peers + mine + 1, devices - 1)
    next_pcoef = lax.dynamic_slice(pay, (next_dev, 8, 0), (1, node_rows, 128)).reshape(nodes)
    scale = jnp.concatenate([pcoef, next_pcoef]).reshape(2 * nodes, 1)

    vec = whole((blocks, size, width), f32)
    emitted = [
        vec,
        vec,
        whole((blocks, size, width), bf16),
        whole((peers, CAP, size, width), bf16),
        whole((nodes, width), bf16),
        whole((nodes, width), bf16),
    ]
    w, z, zb, send, near, far, beta = call(
        start_kernel,
        emitted + [whole((8, width), f32)],
        [VM, VM, SM, SM, VM, VM],
    )(pay, right_side, jacobi_ids, needs, preconditioners, ends)
    basis = [w]
    fields = [z]
    chunk = 16
    while entries % chunk:
        chunk //= 2
    constant = pl.BlockSpec(memory_space=pltpu.VMEM)
    for step in range(ITERS):
        arrived = lax.ppermute(far, "narrow", [(i, i + 1) for i in range(peers - 1)])
        beyond = lax.ppermute(near, "narrow", [(i + 1, i) for i in range(peers - 1)])
        incoming = lax.all_to_all(send, "narrow", 0, 0).reshape(peers * CAP, size, width)
        (part,) = call(
            local_kernel,
            [vec],
            [VM] * 11,
            scratch_shapes=[pltpu.VMEM((2 * nodes, width), bf16)],
        )(z, zb, self_blocks, res_col, freq, near, far, arrived, beyond, scale, ends_col)
        streamed = pl.BlockSpec((chunk, size, size), lambda i: (i, 0, 0))
        common = (rows, slots, couple_blocks, incoming, part, freq)
        specs = [SM, SM, streamed, constant, constant, constant]
        more = dict(
            grid=(entries // chunk,),
            scratch_shapes=[pltpu.VMEM((blocks, size, width), f32)],
        )
        if step + 1 < ITERS:
            w, z, zb, send, near, far = call(
                functools.partial(middle_kernel, chunk),
                emitted,
                specs + [SM, SM, constant, constant],
                **more,
            )(*common, jacobi_ids, needs, preconditioners, ends)
            basis.append(w)
            fields.append(z)
        else:
            (sums,) = call(
                functools.partial(last_kernel, chunk),
                [whole((devices, 16, 128), f32)],
                specs + [constant] * 3,
                **more,
            )(*common, *basis)
    sums = lax.all_to_all(sums, AXES, 0, 0)
    result, norms = call(
        finish_kernel, [vec, whole((8, width), f32)], [VM] * 5
    )(sums, beta, *fields)
    return result, norms[0].reshape(CASES, 2, F)[:, 0, :]


def solution(mesh):
    placed = (
        P(AXES, None, None),
        P(AXES, None),
        P(),
        P(AXES),
        P(AXES, None, None),
        P(AXES, None, None),
        P(None, AXES),
        P(AXES, None, None),
        P(AXES),
        P(),
    )
    return jax.shard_map(
        on_device,
        mesh=mesh,
        in_specs=placed,
        out_specs=(P(AXES, None, None), P()),
        check_vma=False,
    )
```

```python
import functools
import jax
import jax.numpy as jnp
from jax import lax
from jax.experimental import pallas as pl
from jax.experimental.pallas import tpu as pltpu
from jax.sharding import PartitionSpec as P

F = 32
CASES = 2
ITERS = 3
CAP = 4
AXES = ("wide", "narrow")
STEP = 2.0**-8
LIMIT = 40 * 1024 * 1024
QUAD = 4
RUN = 17
f32 = jnp.float32
bf16 = jnp.bfloat16
i32 = jnp.int32
i16 = jnp.int16


def whole(shape, dtype):
    return jax.ShapeDtypeStruct(shape, dtype)


def kept(shape, dtype):
    return pltpu.HBM(shape, dtype)


def in_hbm(value):
    return pltpu.with_memory_space_constraint(value, pltpu.HBM)


def near_core(value):
    return pltpu.with_memory_space_constraint(value, pltpu.VMEM)


VM = pl.BlockSpec(memory_space=pltpu.VMEM)
SM = pl.BlockSpec(memory_space=pltpu.SMEM)
HB = pl.BlockSpec(memory_space=pl.ANY)


def lane_is_real(shape):
    lane = lax.broadcasted_iota(i32, shape, len(shape) - 1)
    return lax.rem(lane, 2 * F) < F


def both_parts(row):
    other = jnp.where(lane_is_real(row.shape), pltpu.roll(row, 128 - F, 1), pltpu.roll(row, F, 1))
    return row + other


def turned(values):
    return jnp.where(
        lane_is_real(values.shape),
        -pltpu.roll(values, 128 - F, 1),
        pltpu.roll(values, F, 1),
    )


def block_ranks(peers, blocks, lists_ref):
    keys = peers * blocks
    entries = lists_ref.shape[1]
    key = lists_ref[2:3, :] * blocks + lists_ref[1:2, :]
    one = (lax.broadcasted_iota(i32, (keys, entries), 0) == key).astype(f32)
    present = jnp.max(one, axis=1, keepdims=True)
    row = lax.broadcasted_iota(i32, (keys, keys), 0)
    col = lax.broadcasted_iota(i32, (keys, keys), 1)
    before = jnp.where((row // blocks == col // blocks) & (col <= row), 1.0, 0.0).astype(bf16)
    rank = jnp.dot(
        before,
        jnp.broadcast_to(present, (keys, 128)).astype(bf16),
        preferred_element_type=f32,
    )
    return one, present, rank


def setup_kernel(peers, blocks, lists_ref, right_ref, pcoef_ref, pay_ref):
    keys = peers * blocks
    _, present, rank = block_ranks(peers, blocks, lists_ref)
    lane = lax.broadcasted_iota(i32, (keys, 128), 1)
    name = lax.broadcasted_iota(i32, (keys, 128), 0)
    chosen = (
        (name // blocks == lane // CAP)
        & (rank == (lane % CAP + 1).astype(f32))
        & (present > 0.0)
    )
    needs = jnp.sum(jnp.where(chosen, (name % blocks).astype(f32), 0.0), axis=0, keepdims=True)
    held = jnp.sum(jnp.where(name // blocks == lane, present, 0.0), axis=0, keepdims=True)
    right = right_ref[...]
    squares = jnp.sum(jnp.sum(right * right, axis=0), axis=0, keepdims=True)
    rows = jnp.concatenate([squares, needs, held, jnp.zeros((5, 128), f32), pcoef_ref[...]], axis=0)
    pay_ref[...] = jnp.broadcast_to(rows[None], pay_ref.shape)


def order_kernel(peers, blocks, lists_ref, order_ref, slot_ref, row_ref):
    entries = lists_ref.shape[1]
    places = order_ref.shape[1]
    quads = row_ref.shape[1]
    one, _, rank = block_ranks(peers, blocks, lists_ref)
    place = jnp.sum(one * (rank[:, :1] - 1.0), axis=0, keepdims=True)
    slot = (lists_ref[2:3, :] * CAP).astype(f32) + place
    mine = (lax.broadcasted_iota(i32, (blocks, entries), 0) == lists_ref[0:1, :]).astype(f32)
    earlier = lax.broadcasted_iota(i32, (entries, entries), 0) < lax.broadcasted_iota(
        i32, (entries, entries), 1
    )
    seen = jnp.dot(
        mine.astype(bf16), jnp.where(earlier, 1.0, 0.0).astype(bf16), preferred_element_type=f32
    )
    turn = jnp.sum(mine * seen, axis=0, keepdims=True).astype(i32)
    count = jnp.sum(mine, axis=1, keepdims=True).astype(i32)
    groups = (count + QUAD - 1) // QUAD
    above = lax.broadcasted_iota(i32, (blocks, blocks), 1) < lax.broadcasted_iota(
        i32, (blocks, blocks), 0
    )
    base = jnp.dot(
        jnp.where(above, 1.0, 0.0).astype(bf16),
        jnp.broadcast_to(groups.astype(f32), (blocks, 128)).astype(bf16),
        preferred_element_type=f32,
    )[:, :1]
    start = jnp.sum(mine * base, axis=0, keepdims=True).astype(i32)
    goal = (start + turn // QUAD) * QUAD + turn % QUAD
    found = (lax.broadcasted_iota(i32, (places, entries), 0) == goal).astype(f32).astype(bf16)
    number = lax.broadcasted_iota(i32, (1, entries), 1).astype(f32)
    facts = jnp.concatenate(
        [number, slot, jnp.ones((1, entries), f32), jnp.zeros((5, entries), f32)], axis=0
    )
    table = lax.dot_general(
        facts.astype(bf16), found, (((1,), (1,)), ((), ())), preferred_element_type=f32
    )
    order_ref[...] = table[0:1, :].astype(i32)
    slot_ref[...] = jnp.where(table[2:3, :] > 0.5, table[1:2, :], float(peers * CAP)).astype(i32)
    quad = lax.broadcasted_iota(i32, (blocks, quads), 1).astype(f32)
    inside = (quad >= base) & (quad < base + groups.astype(f32))
    name = lax.broadcasted_iota(i32, (blocks, quads), 0)
    row_ref[...] = jnp.sum(jnp.where(inside, name.astype(f32), 0.0), axis=0, keepdims=True).astype(i32)


def prepare_kernel(order_ref, couple_ref, sorted_ref, held_ref, sems):
    places = sorted_ref.shape[0]
    piece = RUN * QUAD
    runs = places // piece

    def out(step):
        here = pl.ds(step * piece, piece)
        return pltpu.make_async_copy(held_ref.at[here], sorted_ref.at[here], sems.at[runs])

    for step in range(runs):

        def fetch(i, carry, step=step):
            p = step * piece + i
            pltpu.make_async_copy(
                couple_ref.at[order_ref[0, p]], held_ref.at[p], sems.at[step]
            ).start()
            return carry

        lax.fori_loop(0, piece, fetch, 0)
    for step in range(runs):
        here = held_ref.at[pl.ds(step * piece, piece)]
        pltpu.make_async_copy(here, here, sems.at[step]).wait()
        out(step).start()
    pltpu.make_async_copy(held_ref, sorted_ref, sems.at[runs]).wait()


def signs(node, first, second):
    one = jnp.ones(node.shape, bf16)
    return jnp.where(node == first, one, jnp.where(node == second, -one, jnp.zeros_like(one)))


def charges(ends_ref, zb_ref, start, chunk):
    blocks, size, width = zb_ref.shape
    branches = blocks * size
    node = lax.broadcasted_iota(i32, (16, branches), 0).astype(i16)
    groups = []
    for g in range(chunk // 16):
        row = node + jnp.full((16, branches), start + 16 * g, i32).astype(i16)
        groups.append(signs(row, ends_ref[:16, :], ends_ref[16:, :]))
    return jnp.dot(
        jnp.concatenate(groups, axis=0),
        zb_ref[...].reshape(branches, width),
        preferred_element_type=f32,
    ).astype(bf16)


def emit(
    plan, w_of, ends_ref, jacobi_ref, needs_ref, place_ref, table_ref,
    z_ref, send_ref, own_ref, right_ref, left_ref, extra_refs, zv_ref, zb_ref, sv_ref, sems,
):
    blocks, size, width = zb_ref.shape
    peers, base = sv_ref.shape[:2]
    extra = plan[1] - base
    nodes = right_ref.shape[0] - extra * size
    for n in range(blocks):
        z = jnp.dot(table_ref[jacobi_ref[n]], w_of(n).astype(bf16), preferred_element_type=f32)
        zv_ref[n] = z
        zb_ref[n] = z.astype(bf16)
    save = pltpu.make_async_copy(zv_ref, z_ref, sems.at[0])
    save.start()
    for j in range(peers):
        for s in range(base):
            sv_ref[j, s] = zb_ref[needs_ref[j, s]]
    pack = pltpu.make_async_copy(sv_ref, send_ref, sems.at[1])
    pack.start()
    mine = place_ref[0]
    for s in range(CAP):
        own_ref[s] = zb_ref[needs_ref[mine, s]]
    for distance in range(1, peers):
        for s in range(base, plan[distance]):
            for side in range(2):
                peer = jnp.clip(mine + (distance if side == 0 else -distance), 0, peers - 1)
                block = zb_ref[needs_ref[peer, s]]
                if distance == 1:
                    out = right_ref if side == 0 else left_ref
                    out[pl.ds(nodes + (s - base) * size, size), :] = block
                else:
                    extra_refs[2 * (distance - 2) + side][s - base] = block
    chunk = 512
    while nodes % chunk:
        chunk //= 2
    for part, out in ((0, left_ref), (1, right_ref)):

        def body(step, carry, part=part, out=out):
            start = pl.multiple_of(step * chunk, chunk)
            out[pl.ds(start, chunk), :] = charges(ends_ref, zb_ref, start + part * nodes, chunk)
            return carry

        lax.fori_loop(0, nodes // chunk, body, 0)
    save.wait()
    pack.wait()


def start_kernel(
    plan, pay_ref, side_ref, ends_ref, jacobi_ref, needs_ref, place_ref, table_ref,
    w_ref, beta_ref, z_ref, send_ref, own_ref, right_ref, left_ref, *rest,
):
    extra_refs, (zv_ref, zb_ref, sv_ref, sems) = rest[:-4], rest[-4:]
    total = jnp.sum(pay_ref[:, 0, :], axis=0, keepdims=True)
    beta = jnp.sqrt(both_parts(total))
    beta_ref[...] = jnp.broadcast_to(beta, beta_ref.shape)
    w_ref[...] = side_ref[...] / beta[None]
    emit(
        plan, lambda n: w_ref[n], ends_ref, jacobi_ref, needs_ref, place_ref, table_ref,
        z_ref, send_ref, own_ref, right_ref, left_ref, extra_refs, zv_ref, zb_ref, sv_ref, sems,
    )


def local_kernel(z_ref, self_ref, res_ref, freq_ref, part_ref):
    freq = freq_ref[...]
    for n in range(z_ref.shape[0]):
        z = z_ref[n]
        flux = jnp.dot(self_ref[n], z.astype(bf16), preferred_element_type=f32)
        part_ref[n] = res_ref[n] * z + turned(freq * flux)


def node_drop(cols_ref, scale_ref, left_ref, right_ref, arrived_ref, beyond_ref, drop_ref):
    nodes = scale_ref.shape[1] // 2
    blocks, size, width = drop_ref.shape
    charge = jnp.concatenate(
        [
            left_ref[:nodes].astype(f32) + arrived_ref[:nodes].astype(f32),
            right_ref[:nodes].astype(f32) + beyond_ref[:nodes].astype(f32),
        ],
        axis=0,
    ).astype(bf16)
    group = 4
    while blocks % group:
        group //= 2
    chunk = group * size

    def body(step, carry):
        start = pl.multiple_of(step * chunk, chunk)
        node = lax.broadcasted_iota(i32, (16, 2 * nodes), 1).astype(i16)
        plus = scale_ref[...]
        none = jnp.zeros_like(plus)
        rows = []
        for g in range(chunk // 16):
            ends = cols_ref[pl.ds(start + 16 * g, 16), :]
            rows.append(
                jnp.where(
                    node == ends[:, 0:1], plus, jnp.where(node == ends[:, 1:2], -plus, none)
                )
            )
        drop = jnp.dot(jnp.concatenate(rows, axis=0), charge, preferred_element_type=f32)
        drop_ref[pl.ds(step * group, group)] = drop.reshape(group, size, width)
        return carry

    lax.fori_loop(0, blocks // group, body, 0)


def couple(
    plan, row_ref, slot_ref, place_ref, sorted_ref, incoming_ref, own_ref, arrived_ref, beyond_ref,
    extra_refs, cols_ref, scale_ref, left_ref, right_ref, drop_ref, acc_ref, source_ref, held_ref,
    sems,
):
    places = held_ref.shape[0]
    piece = RUN * QUAD
    runs = places // piece

    def copy(step):
        here = pl.ds(step * piece, piece)
        return pltpu.make_async_copy(sorted_ref.at[here], held_ref.at[here], sems.at[step])

    for step in range(runs):
        copy(step).start()
    peers, base, size, width = incoming_ref.shape
    extra = plan[1] - base
    nodes = arrived_ref.shape[0] - extra * size
    mine = place_ref[0]
    for j in range(peers):
        for s in range(base):
            source_ref[j * CAP + s] = incoming_ref[j, s]
    source_ref[peers * CAP] = jnp.zeros((size, width), bf16)
    for s in range(base, CAP):
        source_ref[mine * CAP + s] = own_ref[s]
    for distance in range(1, peers):
        for s in range(base, plan[distance]):
            for side in range(2):
                peer = mine + (-distance if side == 0 else distance)
                there = (peer >= 0) & (peer < peers)
                slot = jnp.where(there, peer * CAP + s, peers * CAP + 1)
                if distance == 1:
                    source = arrived_ref if side == 0 else beyond_ref
                    block = source[pl.ds(nodes + (s - base) * size, size), :]
                else:
                    block = extra_refs[2 * (distance - 2) + side][s - base]
                source_ref[slot] = block
    acc_ref[...] = jnp.zeros_like(acc_ref)
    node_drop(cols_ref, scale_ref, left_ref, right_ref, arrived_ref, beyond_ref, drop_ref)

    def body(step, carry):
        copy(step).wait()
        for u in range(RUN):
            quad = step * RUN + u
            left = jnp.concatenate([held_ref[quad * QUAD + i] for i in range(QUAD)], axis=1)
            right = jnp.concatenate(
                [source_ref[slot_ref[0, quad * QUAD + i]] for i in range(QUAD)], axis=0
            )
            acc_ref[row_ref[0, quad]] += jnp.dot(left, right, preferred_element_type=f32)
        return carry

    lax.fori_loop(0, runs, body, 0)


def image_of(part_ref, freq_ref, acc_ref, drop_ref, n):
    freq = freq_ref[...]
    return STEP * (part_ref[n] + turned(freq * acc_ref[n] - drop_ref[n] / freq))


def split(plan, rest):
    count = extras(plan)
    return rest[:count], rest[count:]


def extras(plan):
    return 2 * sum(1 for slots in plan[2:] if slots > plan[0])


def middle_kernel(
    plan, row_ref, slot_ref, place_ref, sorted_ref, incoming_ref, own_in_ref, arrived_ref,
    beyond_ref, *rest,
):
    come, rest = split(plan, rest)
    part_ref, freq_ref, cols_ref, scale_ref, left_in_ref, right_in_ref = rest[:6]
    ends_ref, jacobi_ref, needs_ref, table_ref = rest[6:10]
    w_ref, z_ref, send_ref, own_ref, right_ref, left_ref = rest[10:16]
    go, rest = split(plan, rest[16:])
    drop_ref, acc_ref, source_ref, held_ref, run_sems, wv_ref, zv_ref, zb_ref, sv_ref, sems = rest
    couple(
        plan, row_ref, slot_ref, place_ref, sorted_ref, incoming_ref, own_in_ref, arrived_ref,
        beyond_ref, come, cols_ref, scale_ref, left_in_ref, right_in_ref, drop_ref, acc_ref,
        source_ref, held_ref, run_sems,
    )
    for n in range(wv_ref.shape[0]):
        wv_ref[n] = image_of(part_ref, freq_ref, acc_ref, drop_ref, n)
    save = pltpu.make_async_copy(wv_ref, w_ref, sems.at[2])
    save.start()
    emit(
        plan, lambda n: wv_ref[n], ends_ref, jacobi_ref, needs_ref, place_ref, table_ref,
        z_ref, send_ref, own_ref, right_ref, left_ref, go, zv_ref, zb_ref, sv_ref, sems,
    )
    save.wait()


PAIRS = [(i, j) for j in range(ITERS + 1) for i in range(j + 1)]


def last_kernel(
    plan, row_ref, slot_ref, place_ref, sorted_ref, incoming_ref, own_ref, arrived_ref,
    beyond_ref, *rest,
):
    come, rest = split(plan, rest)
    part_ref, freq_ref, cols_ref, scale_ref, left_ref, right_ref = rest[:6]
    w0_ref, w1_ref, w2_ref, pay_ref, drop_ref, acc_ref, source_ref, held_ref, sems = rest[6:]
    couple(
        plan, row_ref, slot_ref, place_ref, sorted_ref, incoming_ref, own_ref, arrived_ref,
        beyond_ref, come, cols_ref, scale_ref, left_ref, right_ref, drop_ref, acc_ref, source_ref,
        held_ref, sems,
    )
    blocks = acc_ref.shape[0]

    def body(n, sums):
        w = [w0_ref[n], w1_ref[n], w2_ref[n], image_of(part_ref, freq_ref, acc_ref, drop_ref, n)]
        fresh = []
        for at, (i, j) in enumerate(PAIRS):
            product = (w[i] * w[j]).reshape(-1, 8, 128)
            fresh.append(sums[at] + jnp.sum(product, axis=0))
        return tuple(fresh)

    sums = lax.fori_loop(0, blocks, body, tuple(jnp.zeros((8, 128), f32) for _ in PAIRS))
    rows = [jnp.sum(s, axis=0, keepdims=True) for s in sums]
    rows.append(jnp.zeros((16 - len(rows), 128), f32))
    pay_ref[...] = jnp.broadcast_to(jnp.concatenate(rows, axis=0)[None], pay_ref.shape)


def finish_kernel(pay_ref, beta_ref, z0_ref, z1_ref, z2_ref, out_ref, norm_ref):
    total = both_parts(jnp.sum(pay_ref[...], axis=0))
    gram = {}
    for at, (i, j) in enumerate(PAIRS):
        gram[i, j] = gram[j, i] = total[at : at + 1, :]
    order = list(range(1, ITERS + 1)) + [0]
    low = {}
    for i in range(ITERS + 1):
        for j in range(i + 1):
            value = gram[order[i], order[j]]
            for k in range(j):
                value = value - low[i, k] * low[j, k]
            low[i, j] = jnp.sqrt(jnp.maximum(value, 0.0)) if i == j else value / low[j, j]
    weights = [None] * ITERS
    for i in reversed(range(ITERS)):
        value = low[ITERS, i]
        for k in range(i + 1, ITERS):
            value = value - low[k, i] * weights[k]
        weights[i] = value / low[i, i]
    beta = beta_ref[0:1, :]
    norm_ref[...] = jnp.broadcast_to(low[ITERS, ITERS] * beta, norm_ref.shape)
    weights = [STEP * beta * weight for weight in weights]
    for n in range(out_ref.shape[0]):
        out_ref[n] = weights[0] * z0_ref[n] + weights[1] * z1_ref[n] + weights[2] * z2_ref[n]


def call(kernel, outs, ins, places=None, **more):
    return pl.pallas_call(
        kernel,
        out_shape=outs,
        in_specs=ins,
        out_specs=places or [VM] * len(outs),
        compiler_params=pltpu.CompilerParams(vmem_limit_bytes=LIMIT),
        **more,
    )


def iterate(
    plan, pay, right_side, jacobi_ids, needs, place, table, ends, ends_col, selfs, res, scale,
    freq, order, sorted_blocks,
):
    slots, rows = order
    peers = needs.shape[0]
    devices = pay.shape[0]
    blocks, size, width = right_side.shape
    nodes = scale.shape[1] // 2
    base = plan[0]
    far = [d for d in range(2, peers) if plan[d] > base]
    halo = kept((nodes + (plan[1] - base) * size, width), bf16)
    vec = kept((blocks, size, width), f32)
    emitted = [
        vec,
        kept((peers, base, size, width), bf16),
        kept((CAP, size, width), bf16),
        halo,
        halo,
    ] + [kept((plan[d] - base, size, width), bf16) for d in far for side in range(2)]
    spots = [HB, HB] + [VM] * (len(emitted) - 2)
    buffers = [
        pltpu.VMEM((blocks, size, width), f32),
        pltpu.VMEM((blocks, size, width), bf16),
        pltpu.VMEM((peers, base, size, width), bf16),
        pltpu.SemaphoreType.DMA((3,)),
    ]
    places = sorted_blocks.shape[0]
    coupling = [
        pltpu.VMEM((blocks, size, width), f32),
        pltpu.VMEM((blocks, size, width), f32),
        pltpu.VMEM((peers * CAP + 2, size, width), bf16),
        pltpu.VMEM((places, size, size), bf16),
        pltpu.SemaphoreType.DMA((places // (RUN * QUAD),)),
    ]
    w, beta, z, send, own, right, left, *go = call(
        functools.partial(start_kernel, plan),
        [vec, whole((8, width), f32)] + emitted,
        [VM, VM, VM, SM, SM, SM, VM],
        [VM, VM] + spots,
        scratch_shapes=buffers,
    )(near_core(pay), right_side, ends, jacobi_ids, needs, place, table)
    basis = [w]
    fields = [z]
    for step in range(ITERS):

        def moved(value, distance):
            route = [(i, i + distance) for i in range(peers) if 0 <= i + distance < peers]
            return near_core(lax.ppermute(value, "narrow", route))

        arrived = moved(right, 1)
        beyond = moved(left, -1)
        come = []
        for at, d in enumerate(far):
            come += [moved(go[2 * at], d), moved(go[2 * at + 1], -d)]
        incoming = near_core(lax.all_to_all(send, "narrow", 0, 0))
        (part,) = call(local_kernel, [vec], [VM] * 4)(in_hbm(z), selfs, res, freq)
        common = (
            rows, slots, place, in_hbm(sorted_blocks), incoming, in_hbm(own), arrived, beyond, *come,
            in_hbm(part), freq, ends_col, scale, in_hbm(left), in_hbm(right),
        )
        specs = [SM, SM, SM, HB] + [VM] * (10 + len(come))
        if step + 1 < ITERS:
            w, z, send, own, right, left, *go = call(
                functools.partial(middle_kernel, plan),
                [vec] + emitted,
                specs + [VM, SM, SM, VM],
                [HB] + spots,
                scratch_shapes=coupling + [pltpu.VMEM((blocks, size, width), f32)] + buffers,
            )(*common, ends, jacobi_ids, needs, table)
            basis.append(w)
            fields.append(z)
        else:
            (sums,) = call(
                functools.partial(last_kernel, plan),
                [whole((devices, 16, 128), f32)],
                specs + [VM] * 3,
                scratch_shapes=coupling,
            )(*common, *map(in_hbm, basis))
    sums = near_core(lax.all_to_all(sums, AXES, 0, 0))
    return call(finish_kernel, [vec, whole((8, width), f32)], [VM] * 5)(sums, beta, *map(in_hbm, fields))


def on_device(
    right_side, resistance, omega, pcoef, branch_nodes, self_blocks, couple_list, couple_blocks,
    jacobi_ids, preconditioners,
):
    blocks, size, width = right_side.shape
    nodes = pcoef.shape[0]
    entries = couple_list.shape[1]
    peers = lax.axis_size("narrow")
    devices = peers * lax.axis_size("wide")
    group = lax.axis_index("wide")
    mine = lax.axis_index("narrow")
    node_rows = nodes // 128
    freq = jnp.tile(omega, 2 * CASES).reshape(1, width)
    pairs = jnp.transpose(branch_nodes, (1, 0, 2)).reshape(2, blocks * size)
    pairs = jnp.where(pairs[0] == pairs[1], -1, pairs)
    ends = jnp.repeat(pairs.astype(i16), 16, axis=0)
    ends_col = jnp.transpose(pairs).astype(i16)
    quads = (entries + (QUAD - 1) * blocks) // QUAD
    quads = -(-quads // RUN) * RUN

    (pay,) = call(
        functools.partial(setup_kernel, peers, blocks),
        [whole((devices, 8 + node_rows, 128), f32)],
        [VM] * 3,
    )(couple_list, in_hbm(right_side), pcoef.reshape(node_rows, 128))
    pay = lax.all_to_all(pay, AXES, 0, 0)
    order, slots, rows = call(
        functools.partial(order_kernel, peers, blocks),
        [whole((1, quads * QUAD), i32), whole((1, quads * QUAD), i32), whole((1, quads), i32)],
        [VM],
    )(couple_list)
    (sorted_blocks,) = call(
        prepare_kernel,
        [kept((quads * QUAD, size, size), bf16)],
        [SM, HB],
        [HB],
        scratch_shapes=[
            pltpu.VMEM((quads * QUAD, size, size), bf16),
            pltpu.SemaphoreType.DMA((quads // RUN + 1,)),
        ],
    )(order, in_hbm(couple_blocks))
    needs = lax.dynamic_slice(
        pay, (group * peers, 1, mine * CAP), (peers, 1, CAP)
    ).reshape(peers, CAP).astype(i32)
    next_dev = jnp.minimum(group * peers + mine + 1, devices - 1)
    next_pcoef = lax.dynamic_slice(pay, (next_dev, 8, 0), (1, node_rows, 128)).reshape(nodes)
    scale = jnp.concatenate([pcoef, next_pcoef]).astype(bf16)
    scale = jnp.broadcast_to(scale[None], (16, 2 * nodes))
    shared = (
        pay, in_hbm(right_side), jacobi_ids, needs, mine.reshape(1), in_hbm(preconditioners),
        in_hbm(ends), in_hbm(ends_col), in_hbm(self_blocks),
        in_hbm(resistance.reshape(blocks, size, 1)), in_hbm(scale), freq, (slots, rows),
        sorted_blocks,
    )
    full = (CAP,) * peers
    near = (1,) + tuple(max(1, CAP // distance) for distance in range(1, peers))
    place = jnp.arange(devices) % peers
    reach = jnp.abs(place[:, None] - jnp.arange(peers)[None, :])
    allowed = jnp.where(reach == 0, CAP, jnp.asarray(near, f32)[reach])
    fits = jnp.all(pay[:, 2, :peers] <= allowed)
    result, norms = lax.cond(
        fits, lambda given: iterate(near, *given), lambda given: iterate(full, *given), shared
    )
    return result, norms[0].reshape(CASES, 2, F)[:, 0, :]


def solution(mesh):
    placed = (
        P(AXES, None, None),
        P(AXES, None),
        P(),
        P(AXES),
        P(AXES, None, None),
        P(AXES, None, None),
        P(None, AXES),
        P(AXES, None, None),
        P(AXES),
        P(),
    )
    return jax.shard_map(
        on_device,
        mesh=mesh,
        in_specs=placed,
        out_specs=(P(AXES, None, None), P()),
        check_vma=False,
    )
```

```python
import functools
import jax
import jax.numpy as jnp
import numpy as np
from jax import lax
from jax.experimental import pallas as pl
from jax.experimental.pallas import tpu as pltpu
from jax.sharding import PartitionSpec as P

F = 32
CASES = 2
ITERS = 3
CAP = 4
AXES = ("wide", "narrow")
STEP = 2.0**-8
LIMIT = 40 * 1024 * 1024
QUAD = 4
RUN = 17
WEIGHT = 64
NODE_ROW = 128
PAD = 2
f32 = jnp.float32
bf16 = jnp.bfloat16
i32 = jnp.int32
i16 = jnp.int16


def whole(shape, dtype):
    return jax.ShapeDtypeStruct(shape, dtype)


def kept(shape, dtype):
    return pltpu.HBM(shape, dtype)


def in_hbm(value):
    return pltpu.with_memory_space_constraint(value, pltpu.HBM)


def near_core(value):
    return pltpu.with_memory_space_constraint(value, pltpu.VMEM)


VM = pl.BlockSpec(memory_space=pltpu.VMEM)
SM = pl.BlockSpec(memory_space=pltpu.SMEM)
HB = pl.BlockSpec(memory_space=pl.ANY)


def lane_is_real(shape):
    lane = lax.broadcasted_iota(i32, shape, len(shape) - 1)
    return lax.rem(lane, 2 * F) < F


def both_parts(row):
    other = jnp.where(lane_is_real(row.shape), pltpu.roll(row, 128 - F, 1), pltpu.roll(row, F, 1))
    return row + other


def turned(values):
    return jnp.where(
        lane_is_real(values.shape),
        -pltpu.roll(values, 128 - F, 1),
        pltpu.roll(values, F, 1),
    )


def block_ranks(peers, blocks, lists_ref):
    keys = peers * blocks
    entries = lists_ref.shape[1]
    key = lists_ref[2:3, :] * blocks + lists_ref[1:2, :]
    one = (lax.broadcasted_iota(i32, (keys, entries), 0) == key).astype(f32)
    present = jnp.max(one, axis=1, keepdims=True)
    row = lax.broadcasted_iota(i32, (keys, keys), 0)
    col = lax.broadcasted_iota(i32, (keys, keys), 1)
    before = jnp.where((row // blocks == col // blocks) & (col <= row), 1.0, 0.0).astype(bf16)
    rank = jnp.dot(
        before,
        jnp.broadcast_to(present, (keys, 128)).astype(bf16),
        preferred_element_type=f32,
    )
    return one, present, rank


def setup_kernel(peers, blocks, lists_ref, right_ref, pay_ref):
    keys = peers * blocks
    _, present, rank = block_ranks(peers, blocks, lists_ref)
    lane = lax.broadcasted_iota(i32, (keys, 128), 1)
    name = lax.broadcasted_iota(i32, (keys, 128), 0)
    chosen = (
        (name // blocks == lane // CAP)
        & (rank == (lane % CAP + 1).astype(f32))
        & (present > 0.0)
    )
    needs = jnp.sum(jnp.where(chosen, (name % blocks).astype(f32), 0.0), axis=0, keepdims=True)
    held = jnp.sum(jnp.where(name // blocks == lane, present, 0.0), axis=0, keepdims=True)
    right = right_ref[...]
    squares = jnp.sum(jnp.sum(right * right, axis=0), axis=0, keepdims=True)
    rows = jnp.concatenate([squares, needs, held, jnp.zeros((5, 128), f32)], axis=0)
    pay_ref[...] = jnp.broadcast_to(rows[None], pay_ref.shape)


def order_kernel(peers, blocks, lists_ref, order_ref, slot_ref, row_ref):
    entries = lists_ref.shape[1]
    places = order_ref.shape[1]
    quads = row_ref.shape[1]
    one, _, rank = block_ranks(peers, blocks, lists_ref)
    place = jnp.sum(one * (rank[:, :1] - 1.0), axis=0, keepdims=True)
    slot = (lists_ref[2:3, :] * CAP).astype(f32) + place
    mine = (lax.broadcasted_iota(i32, (blocks, entries), 0) == lists_ref[0:1, :]).astype(f32)
    earlier = lax.broadcasted_iota(i32, (entries, entries), 0) < lax.broadcasted_iota(
        i32, (entries, entries), 1
    )
    seen = jnp.dot(
        mine.astype(bf16), jnp.where(earlier, 1.0, 0.0).astype(bf16), preferred_element_type=f32
    )
    turn = jnp.sum(mine * seen, axis=0, keepdims=True).astype(i32)
    count = jnp.sum(mine, axis=1, keepdims=True).astype(i32)
    groups = (count + QUAD - 1) // QUAD
    above = lax.broadcasted_iota(i32, (blocks, blocks), 1) < lax.broadcasted_iota(
        i32, (blocks, blocks), 0
    )
    base = jnp.dot(
        jnp.where(above, 1.0, 0.0).astype(bf16),
        jnp.broadcast_to(groups.astype(f32), (blocks, 128)).astype(bf16),
        preferred_element_type=f32,
    )[:, :1]
    start = jnp.sum(mine * base, axis=0, keepdims=True).astype(i32)
    goal = (start + turn // QUAD) * QUAD + turn % QUAD
    found = (lax.broadcasted_iota(i32, (places, entries), 0) == goal).astype(f32).astype(bf16)
    number = lax.broadcasted_iota(i32, (1, entries), 1).astype(f32)
    facts = jnp.concatenate(
        [number, slot, jnp.ones((1, entries), f32), jnp.zeros((5, entries), f32)], axis=0
    )
    table = lax.dot_general(
        facts.astype(bf16), found, (((1,), (1,)), ((), ())), preferred_element_type=f32
    )
    order_ref[...] = table[0:1, :].astype(i32)
    slot_ref[...] = jnp.where(table[2:3, :] > 0.5, table[1:2, :], float(peers * CAP)).astype(i32)
    quad = lax.broadcasted_iota(i32, (blocks, quads), 1).astype(f32)
    inside = (quad >= base) & (quad < base + groups.astype(f32))
    name = lax.broadcasted_iota(i32, (blocks, quads), 0)
    row_ref[...] = jnp.sum(jnp.where(inside, name.astype(f32), 0.0), axis=0, keepdims=True).astype(i32)


def signs(node, first, second):
    one = jnp.ones(node.shape, bf16)
    return jnp.where(node == first, one, jnp.where(node == second, -one, jnp.zeros_like(one)))


def charges(ends_ref, zb_ref, start, chunk):
    blocks, size, width = zb_ref.shape
    branches = blocks * size
    node = lax.broadcasted_iota(i32, (16, branches), 0).astype(i16)
    groups = []
    for g in range(chunk // 16):
        row = node + jnp.full((16, branches), start + 16 * g, i32).astype(i16)
        groups.append(signs(row, ends_ref[:16, :], ends_ref[16:, :]))
    return jnp.dot(
        jnp.concatenate(groups, axis=0),
        zb_ref[...].reshape(branches, width),
        preferred_element_type=f32,
    ).astype(bf16)


def emit(
    plan, w_of, ends_ref, jacobi_ref, needs_ref, place_ref, table_ref, rows_ref,
    z_ref, zb_out_ref, right_ref, left_ref, zv_ref, zb_ref, both_ref, sems,
):
    blocks, size, width = zb_ref.shape
    peers = needs_ref.shape[0]
    base = plan[0]
    node_rows = rows_ref.shape[0]
    nodes = right_ref.shape[0] - (plan[1] - base) * size - node_rows
    for n in range(blocks):
        z = jnp.dot(table_ref[jacobi_ref[n]], w_of(n).astype(bf16), preferred_element_type=f32)
        zv_ref[n] = z
        zb_ref[n] = z.astype(bf16)
    pack = pltpu.make_async_copy(zb_ref, zb_out_ref, sems.at[1])
    pack.start()
    save = pltpu.make_async_copy(zv_ref, z_ref, sems.at[0])
    save.start()
    mine = place_ref[0]
    left_ref[pl.ds(nodes, node_rows), :] = rows_ref[...]
    right_ref[pl.ds(nodes, node_rows), :] = rows_ref[...]
    for s in range(base, plan[1]):
        for out, step in ((right_ref, 1), (left_ref, -1)):
            peer = jnp.clip(mine + step, 0, peers - 1)
            there = nodes + node_rows + (s - base) * size
            out[pl.ds(there, size), :] = zb_ref[needs_ref[peer, s]]
    chunk = nodes if base < CAP else 128

    def body(step, carry):
        start = pl.multiple_of(step * chunk, chunk)
        both_ref[pl.ds(start, chunk), :] = charges(ends_ref, zb_ref, start, chunk)
        return carry

    lax.fori_loop(0, 2 * nodes // chunk, body, 0)
    left_ref[pl.ds(0, nodes), :] = both_ref[pl.ds(0, nodes), :]
    right_ref[pl.ds(0, nodes), :] = both_ref[pl.ds(nodes, nodes), :]
    save.wait()
    pack.wait()


def pack_kernel(plan, needs_ref, place_ref, zb_ref, send_ref, own_ref, *extra_refs):
    peers, base = send_ref.shape[:2]
    mine = place_ref[0]
    for j in range(peers):
        for s in range(base):
            send_ref[j, s] = zb_ref[needs_ref[j, s]]
    for s in range(CAP):
        own_ref[s] = zb_ref[needs_ref[mine, s]]
    at = 0
    for distance in range(2, peers):
        if plan[distance] > base:
            for step in (distance, -distance):
                peer = jnp.clip(mine + step, 0, peers - 1)
                for s in range(base, plan[distance]):
                    extra_refs[at][s - base] = zb_ref[needs_ref[peer, s]]
                at += 1


def start_kernel(
    plan, pay_ref, side_ref, ends_ref, jacobi_ref, needs_ref, place_ref, table_ref, rows_ref,
    w_ref, beta_ref, z_ref, zb_out_ref, right_ref, left_ref, zv_ref, zb_ref, both_ref, sems,
):
    total = jnp.sum(pay_ref[:, 0, :], axis=0, keepdims=True)
    beta = jnp.sqrt(both_parts(total))
    beta_ref[...] = jnp.broadcast_to(beta, beta_ref.shape)
    w_ref[...] = side_ref[...] / beta[None]
    emit(
        plan, lambda n: w_ref[n], ends_ref, jacobi_ref, needs_ref, place_ref, table_ref, rows_ref,
        z_ref, zb_out_ref, right_ref, left_ref, zv_ref, zb_ref, both_ref, sems,
    )


def local_kernel(z_ref, self_ref, res_ref, freq_ref, part_ref):
    freq = freq_ref[...]
    for n in range(z_ref.shape[0]):
        z = z_ref[n]
        flux = jnp.dot(self_ref[n], z.astype(bf16), preferred_element_type=f32)
        part_ref[n] = freq * flux - turned(res_ref[n] * z)


def drop_kernel(
    part_ref, freq_ref, cols_ref, rows_ref, left_ref, right_ref, arrived_ref, beyond_ref, out_ref,
    charge_ref, plus_ref,
):
    node_rows = rows_ref.shape[0]
    group, size, width = out_ref.shape
    nodes = NODE_ROW * node_rows // PAD

    @pl.when(pl.program_id(0) == 0)
    def _():
        charge_ref[:nodes] = (
            left_ref[:nodes].astype(f32) + arrived_ref[:nodes].astype(f32)
        ).astype(bf16)
        charge_ref[nodes:] = (
            right_ref[:nodes].astype(f32) + beyond_ref[:nodes].astype(f32)
        ).astype(bf16)
        own = rows_ref[...].astype(f32)
        next_rows = beyond_ref[pl.ds(nodes, node_rows), :].astype(f32)
        lanes = [own[i : i + 1, :] for i in range(nodes // NODE_ROW)]
        lanes += [next_rows[i : i + 1, :] for i in range(nodes // NODE_ROW)]
        row = jnp.concatenate(lanes, axis=1)
        plus_ref[...] = jnp.broadcast_to(row, (16, 2 * nodes)).astype(bf16)

    plus = plus_ref[...]
    node = lax.broadcasted_iota(i32, (16, 2 * nodes), 1).astype(i16)
    none = jnp.zeros_like(plus)
    rows = []
    for g in range(group * size // 16):
        ends = cols_ref[pl.ds(16 * g, 16), :]
        rows.append(
            jnp.where(node == ends[:, 0:1], plus, jnp.where(node == ends[:, 1:2], -plus, none))
        )
    drop = jnp.dot(jnp.concatenate(rows, axis=0), charge_ref[...], preferred_element_type=f32)
    out_ref[...] = part_ref[...] - (drop / freq_ref[...]).reshape(group, size, width)


def couple(
    plan, order_ref, row_ref, slot_ref, place_ref, blocks_ref, incoming_ref, own_ref, arrived_ref,
    beyond_ref, extra_refs, acc_ref, source_ref, held_ref, sems, later,
):
    places = held_ref.shape[0]
    piece = RUN * QUAD
    runs = places // piece

    def copy(step):
        here = pl.ds(step * piece, piece)
        source = held_ref if order_ref is not None else blocks_ref
        return pltpu.make_async_copy(source.at[here], held_ref.at[here], sems.at[step])

    for step in range(runs):
        if order_ref is None:
            copy(step).start()
            continue

        def fetch(i, carry, step=step):
            p = step * piece + i
            pltpu.make_async_copy(
                blocks_ref.at[order_ref[0, p]], held_ref.at[p], sems.at[step]
            ).start()
            return carry

        lax.fori_loop(0, piece, fetch, 0, unroll=4)
    for fetched in later:
        fetched.start()
    peers, base, size, width = incoming_ref.shape
    extra = plan[1] - base
    head = arrived_ref.shape[0] - extra * size
    mine = place_ref[0]
    for j in range(peers):
        for s in range(base):
            source_ref[j * CAP + s] = incoming_ref[j, s]
    source_ref[peers * CAP] = jnp.zeros((size, width), bf16)
    for s in range(base, CAP):
        source_ref[mine * CAP + s] = own_ref[s]
    for distance in range(1, peers):
        for s in range(base, plan[distance]):
            for side in range(2):
                peer = mine + (-distance if side == 0 else distance)
                there = (peer >= 0) & (peer < peers)
                slot = jnp.where(there, peer * CAP + s, peers * CAP + 1)
                if distance == 1:
                    source = arrived_ref if side == 0 else beyond_ref
                    block = source[pl.ds(head + (s - base) * size, size), :]
                else:
                    block = extra_refs[2 * (distance - 2) + side][s - base]
                source_ref[slot] = block
    acc_ref[...] = jnp.zeros_like(acc_ref)

    def body(step, carry):
        copy(step).wait()
        for u in range(RUN):
            quad = step * RUN + u
            left = jnp.concatenate([held_ref[quad * QUAD + i] for i in range(QUAD)], axis=1)
            right = jnp.concatenate(
                [source_ref[slot_ref[0, quad * QUAD + i]] for i in range(QUAD)], axis=0
            )
            acc_ref[row_ref[0, quad]] += jnp.dot(left, right, preferred_element_type=f32)
        return carry

    lax.fori_loop(0, runs, body, 0)
    for fetched in later:
        fetched.wait()


def image_of(part_ref, freq_ref, acc_ref, n):
    return STEP * turned(part_ref[n] + freq_ref[...] * acc_ref[n])


def split(plan, rest):
    count = extras(plan)
    return rest[:count], rest[count:]


def extras(plan):
    return 2 * sum(1 for slots in plan[2:] if slots > plan[0])


def middle_kernel(
    plan, first, row_ref, slot_ref, place_ref, blocks_ref, incoming_ref, own_ref, arrived_ref,
    beyond_ref, *rest,
):
    come, rest = split(plan, rest)
    part_ref, freq_ref, ends_ref, jacobi_ref, needs_ref, table_ref, rows_ref = rest[:7]
    rest = rest[7:]
    order_ref = None
    if first:
        order_ref, rest = rest[0], rest[1:]
    w_ref, z_ref, zb_out_ref, right_ref, left_ref = rest[:5]
    rest = rest[5:]
    if first:
        sorted_ref, rest = rest[0], rest[1:]
    acc_ref, source_ref, held_ref, run_sems, wv_ref, zv_ref, zb_ref, both_ref, sems = rest
    bring = pltpu.make_async_copy(part_ref, zv_ref, sems.at[0])
    couple(
        plan, order_ref, row_ref, slot_ref, place_ref, blocks_ref, incoming_ref, own_ref,
        arrived_ref, beyond_ref, come, acc_ref, source_ref, held_ref, run_sems, [bring],
    )
    if first:
        keep = pltpu.make_async_copy(held_ref, sorted_ref, sems.at[3])
        keep.start()
    for n in range(wv_ref.shape[0]):
        wv_ref[n] = image_of(zv_ref, freq_ref, acc_ref, n)
    save = pltpu.make_async_copy(wv_ref, w_ref, sems.at[2])
    save.start()
    emit(
        plan, lambda n: wv_ref[n], ends_ref, jacobi_ref, needs_ref, place_ref, table_ref, rows_ref,
        z_ref, zb_out_ref, right_ref, left_ref, zv_ref, zb_ref, both_ref, sems,
    )
    save.wait()
    if first:
        keep.wait()


PAIRS = [(i, j) for j in range(ITERS + 1) for i in range(j + 1)]


def last_kernel(
    plan, row_ref, slot_ref, place_ref, blocks_ref, incoming_ref, own_ref, arrived_ref,
    beyond_ref, *rest,
):
    come, rest = split(plan, rest)
    part_ref, freq_ref, w0_ref, w1_ref, w2_ref, pay_ref = rest[:6]
    acc_ref, source_ref, held_ref, run_sems, store_ref, sems = rest[6:]
    bring = [
        pltpu.make_async_copy(source, store_ref.at[at], sems.at[at])
        for at, source in enumerate((part_ref, w0_ref, w1_ref, w2_ref))
    ]
    couple(
        plan, None, row_ref, slot_ref, place_ref, blocks_ref, incoming_ref, own_ref,
        arrived_ref, beyond_ref, come, acc_ref, source_ref, held_ref, run_sems, bring,
    )
    blocks = acc_ref.shape[0]

    def body(n, sums):
        w = [store_ref[1 + k, n] for k in range(ITERS)]
        w.append(image_of(store_ref.at[0], freq_ref, acc_ref, n))
        fresh = []
        for at, (i, j) in enumerate(PAIRS):
            product = (w[i] * w[j]).reshape(-1, 8, 128)
            fresh.append(sums[at] + jnp.sum(product, axis=0))
        return tuple(fresh)

    sums = lax.fori_loop(0, blocks, body, tuple(jnp.zeros((8, 128), f32) for _ in PAIRS))
    rows = [jnp.sum(s, axis=0, keepdims=True) for s in sums]
    rows = [both_parts(row) for row in rows]
    real = lane_is_real((1, 128))
    rows = [jnp.where(real, rows[k], rows[k + 1]) for k in range(0, len(rows), 2)]
    rows.append(jnp.zeros((8 - len(rows), 128), f32))
    pay_ref[...] = jnp.broadcast_to(jnp.concatenate(rows, axis=0)[None], pay_ref.shape)


def finish_kernel(pay_ref, beta_ref, z0_ref, z1_ref, z2_ref, out_ref, norm_ref):
    total = jnp.sum(pay_ref[...], axis=0)
    real = lane_is_real(total.shape)
    even = jnp.where(real, total, pltpu.roll(total, F, 1))
    odd = jnp.where(real, pltpu.roll(total, 128 - F, 1), total)
    gram = {}
    for at, (i, j) in enumerate(PAIRS):
        half = at // 2
        gram[i, j] = gram[j, i] = (odd if at % 2 else even)[half : half + 1, :]
    order = list(range(1, ITERS + 1)) + [0]
    low = {}
    for i in range(ITERS + 1):
        for j in range(i + 1):
            value = gram[order[i], order[j]]
            for k in range(j):
                value = value - low[i, k] * low[j, k]
            low[i, j] = jnp.sqrt(jnp.maximum(value, 0.0)) if i == j else value / low[j, j]
    weights = [None] * ITERS
    for i in reversed(range(ITERS)):
        value = low[ITERS, i]
        for k in range(i + 1, ITERS):
            value = value - low[k, i] * weights[k]
        weights[i] = value / low[i, i]
    beta = beta_ref[0:1, :]
    norm_ref[...] = jnp.broadcast_to(low[ITERS, ITERS] * beta, norm_ref.shape)
    weights = [STEP * beta * weight for weight in weights]
    for n in range(out_ref.shape[0]):
        out_ref[n] = weights[0] * z0_ref[n] + weights[1] * z1_ref[n] + weights[2] * z2_ref[n]


def call(kernel, outs, ins, places=None, **more):
    return pl.pallas_call(
        kernel,
        out_shape=outs,
        in_specs=ins,
        out_specs=places or [VM] * len(outs),
        compiler_params=pltpu.CompilerParams(vmem_limit_bytes=LIMIT),
        **more,
    )


def iterate(
    plan, pay, right_side, jacobi_ids, needs, place, table, ends, ends_col, selfs, res, scale,
    freq, tables, couple_blocks,
):
    order, slots, rows = tables
    peers = needs.shape[0]
    devices = pay.shape[0]
    blocks, size, width = right_side.shape
    nodes = NODE_ROW * scale.shape[0] // PAD
    base = plan[0]
    far = [d for d in range(2, peers) if plan[d] > base]
    halo = kept((nodes + scale.shape[0] + (plan[1] - base) * size, width), bf16)
    vec = kept((blocks, size, width), f32)
    emitted = [vec, kept((blocks, size, width), bf16), halo, halo]
    packed = [
        kept((peers, base, size, width), bf16),
        kept((CAP, size, width), bf16),
    ] + [kept((plan[d] - base, size, width), bf16) for d in far for side in range(2)]
    spots = [HB, HB, VM, VM]
    buffers = [
        pltpu.VMEM((blocks, size, width), f32),
        pltpu.VMEM((blocks, size, width), bf16),
        pltpu.VMEM((2 * nodes, width), bf16),
        pltpu.SemaphoreType.DMA((4,)),
    ]
    places = order.shape[1]
    coupling = [
        pltpu.VMEM((blocks, size, width), f32),
        pltpu.VMEM((peers * CAP + 2, size, width), bf16),
        pltpu.VMEM((places, size, size), bf16),
        pltpu.SemaphoreType.DMA((places // (RUN * QUAD),)),
    ]
    w, beta, z, zb, right, left = call(
        functools.partial(start_kernel, plan),
        [vec, whole((8, width), f32)] + emitted,
        [VM, VM, VM, SM, SM, SM, VM, VM],
        [VM, VM] + spots,
        scratch_shapes=buffers,
    )(near_core(pay), right_side, ends, jacobi_ids, needs, place, table, scale)
    basis = [w]
    fields = [z]
    for step in range(ITERS):

        def moved(value, distance):
            route = [(i, i + distance) for i in range(peers) if 0 <= i + distance < peers]
            return near_core(lax.ppermute(value, "narrow", route))

        arrived = moved(right, 1)
        beyond = moved(left, -1)
        send, own, *go = call(functools.partial(pack_kernel, plan), packed, [SM, SM, VM])(
            needs, place, in_hbm(zb)
        )
        come = []
        for at, d in enumerate(far):
            come += [moved(go[2 * at], d), moved(go[2 * at + 1], -d)]
        incoming = near_core(lax.all_to_all(send, "narrow", 0, 0))
        later, send = lax.optimization_barrier((z, send))
        (part,) = call(local_kernel, [vec], [VM] * 4)(in_hbm(later), selfs, res, freq)
        parts = 2 if base < CAP else blocks
        half = blocks // parts
        block = pl.BlockSpec((half, size, width), lambda i: (i, 0, 0))
        (part,) = call(
            drop_kernel,
            [vec],
            [block, VM, pl.BlockSpec((half * size, 2), lambda i: (i, 0))] + [VM] * 5,
            [block],
            grid=(parts,),
            scratch_shapes=[
                pltpu.VMEM((2 * nodes, width), bf16),
                pltpu.VMEM((16, 2 * nodes), bf16),
            ],
            cost_estimate=pl.CostEstimate(
                flops=WEIGHT * blocks * size * nodes * width,
                bytes_accessed=WEIGHT * blocks * size * width,
                transcendentals=0,
            ),
        )(in_hbm(part), freq, ends_col, scale, in_hbm(left), in_hbm(right), arrived, beyond)
        first = step == 0
        held = couple_blocks if first else sorted_blocks
        common = (
            rows, slots, place, in_hbm(held), incoming, in_hbm(own), arrived, beyond, *come,
            in_hbm(part), freq,
        )
        specs = [SM, SM, SM, HB] + [VM] * (4 + len(come)) + [HB, VM]
        if step + 1 < ITERS:
            w, z, zb, right, left, *copies = call(
                functools.partial(middle_kernel, plan, first),
                [vec] + emitted + ([kept((places, size, size), bf16)] if first else []),
                specs + [VM, SM, SM, VM, VM] + ([SM] if first else []),
                [HB] + spots + ([HB] if first else []),
                scratch_shapes=coupling + [pltpu.VMEM((blocks, size, width), f32)] + buffers,
            )(*common, ends, jacobi_ids, needs, table, scale, *([order] if first else []))
            if first:
                (sorted_blocks,) = copies
            basis.append(w)
            fields.append(z)
        else:
            (sums,) = call(
                functools.partial(last_kernel, plan),
                [whole((devices, 8, 128), f32)],
                specs + [HB] * 3,
                scratch_shapes=coupling
                + [
                    pltpu.VMEM((ITERS + 1, blocks, size, width), f32),
                    pltpu.SemaphoreType.DMA((ITERS + 1,)),
                ],
            )(*common, *map(in_hbm, basis))
    sums = near_core(lax.all_to_all(sums, AXES, 0, 0))
    return call(finish_kernel, [vec, whole((8, width), f32)], [VM] * 5)(
        sums, beta, *map(in_hbm, fields)
    )


def on_device(
    right_side, resistance, omega, pcoef, branch_nodes, self_blocks, couple_list, couple_blocks,
    jacobi_ids, preconditioners,
):
    blocks, size, width = right_side.shape
    nodes = pcoef.shape[0]
    entries = couple_list.shape[1]
    peers = lax.axis_size("narrow")
    devices = peers * lax.axis_size("wide")
    group = lax.axis_index("wide")
    mine = lax.axis_index("narrow")
    node_rows = nodes // NODE_ROW
    freq = jnp.tile(omega, 2 * CASES).reshape(1, width)
    pairs = jnp.transpose(branch_nodes, (1, 0, 2)).reshape(2, blocks * size)
    pairs = jnp.where(pairs[0] == pairs[1], -1, pairs)
    ends = jnp.repeat(pairs.astype(i16), 16, axis=0)
    ends_col = jnp.transpose(pairs).astype(i16)
    quads = (entries + (QUAD - 1) * blocks) // QUAD
    quads = -(-quads // RUN) * RUN

    (pay,) = call(
        functools.partial(setup_kernel, peers, blocks),
        [whole((devices, 8, 128), f32)],
        [VM] * 2,
    )(couple_list, in_hbm(right_side))
    pay = lax.all_to_all(pay, AXES, 0, 0)
    order, slots, rows = call(
        functools.partial(order_kernel, peers, blocks),
        [whole((1, quads * QUAD), i32), whole((1, quads * QUAD), i32), whole((1, quads), i32)],
        [VM],
    )(couple_list)
    needs = lax.dynamic_slice(
        pay, (group * peers, 1, mine * CAP), (peers, 1, CAP)
    ).reshape(peers, CAP).astype(i32)
    rows16 = jnp.pad(pcoef.astype(bf16).reshape(node_rows, 128), ((0, node_rows), (0, 0)))
    shared = (
        pay, in_hbm(right_side), jacobi_ids, needs, mine.reshape(1), in_hbm(preconditioners),
        in_hbm(ends), in_hbm(ends_col), in_hbm(self_blocks),
        in_hbm(resistance.reshape(blocks, size, 1)), in_hbm(rows16), freq, (order, slots, rows),
        in_hbm(couple_blocks),
    )
    full = (CAP,) * peers
    near = (2,) + tuple(max(2, CAP // distance) for distance in range(1, peers))
    reach = np.abs(np.arange(devices)[:, None] % peers - np.arange(peers)[None, :])
    allowed = np.where(reach == 0, CAP, np.asarray(near)[reach]).astype(np.float32)
    fits = jnp.all(pay[:, 2, :peers] <= allowed)
    result, norms = lax.cond(
        fits, lambda given: iterate(near, *given), lambda given: iterate(full, *given), shared
    )
    return result, norms[0].reshape(CASES, 2, F)[:, 0, :]


def solution(mesh):
    placed = (
        P(AXES, None, None),
        P(AXES, None),
        P(),
        P(AXES),
        P(AXES, None, None),
        P(AXES, None, None),
        P(None, AXES),
        P(AXES, None, None),
        P(AXES),
        P(),
    )
    return jax.shard_map(
        on_device,
        mesh=mesh,
        in_specs=placed,
        out_specs=(P(AXES, None, None), P()),
        check_vma=False,
    )
```

```python
import functools
import jax
import jax.numpy as jnp
import numpy as np
from jax import lax
from jax.experimental import pallas as pl
from jax.experimental.pallas import tpu as pltpu
from jax.sharding import PartitionSpec as P

F = 32
CASES = 2
ITERS = 3
CAP = 4
AXES = ("wide", "narrow")
STEP = 2.0**-8
LIMIT = 40 * 1024 * 1024
QUAD = 4
RUN = 17
WEIGHT = 64
NODE_ROW = 128
PAD = 2
f32 = jnp.float32
bf16 = jnp.bfloat16
i32 = jnp.int32
i16 = jnp.int16


def whole(shape, dtype):
    return jax.ShapeDtypeStruct(shape, dtype)


def kept(shape, dtype):
    return pltpu.HBM(shape, dtype)


def in_hbm(value):
    return pltpu.with_memory_space_constraint(value, pltpu.HBM)


def near_core(value):
    return pltpu.with_memory_space_constraint(value, pltpu.VMEM)


VM = pl.BlockSpec(memory_space=pltpu.VMEM)
SM = pl.BlockSpec(memory_space=pltpu.SMEM)
HB = pl.BlockSpec(memory_space=pl.ANY)


def lane_is_real(shape):
    lane = lax.broadcasted_iota(i32, shape, len(shape) - 1)
    return lax.rem(lane, 2 * F) < F


def both_parts(row):
    other = jnp.where(lane_is_real(row.shape), pltpu.roll(row, 128 - F, 1), pltpu.roll(row, F, 1))
    return row + other


def turned(values):
    return jnp.where(
        lane_is_real(values.shape),
        -pltpu.roll(values, 128 - F, 1),
        pltpu.roll(values, F, 1),
    )


def block_ranks(peers, blocks, lists_ref):
    keys = peers * blocks
    entries = lists_ref.shape[1]
    key = lists_ref[2:3, :] * blocks + lists_ref[1:2, :]
    one = (lax.broadcasted_iota(i32, (keys, entries), 0) == key).astype(f32)
    present = jnp.max(one, axis=1, keepdims=True)
    row = lax.broadcasted_iota(i32, (keys, keys), 0)
    col = lax.broadcasted_iota(i32, (keys, keys), 1)
    before = jnp.where((row // blocks == col // blocks) & (col <= row), 1.0, 0.0).astype(bf16)
    rank = jnp.dot(
        before,
        jnp.broadcast_to(present, (keys, 128)).astype(bf16),
        preferred_element_type=f32,
    )
    return one, present, rank


def setup_kernel(peers, blocks, lists_ref, right_ref, pay_ref):
    keys = peers * blocks
    _, present, rank = block_ranks(peers, blocks, lists_ref)
    lane = lax.broadcasted_iota(i32, (keys, 128), 1)
    name = lax.broadcasted_iota(i32, (keys, 128), 0)
    chosen = (
        (name // blocks == lane // CAP)
        & (rank == (lane % CAP + 1).astype(f32))
        & (present > 0.0)
    )
    needs = jnp.sum(jnp.where(chosen, (name % blocks).astype(f32), 0.0), axis=0, keepdims=True)
    held = jnp.sum(jnp.where(name // blocks == lane, present, 0.0), axis=0, keepdims=True)
    right = right_ref[...]
    squares = jnp.sum(jnp.sum(right * right, axis=0), axis=0, keepdims=True)
    rows = jnp.concatenate([squares, needs, held, jnp.zeros((5, 128), f32)], axis=0)
    pay_ref[...] = jnp.broadcast_to(rows[None], pay_ref.shape)


def order_kernel(peers, blocks, lists_ref, order_ref, slot_ref, row_ref):
    entries = lists_ref.shape[1]
    places = order_ref.shape[1]
    quads = row_ref.shape[1]
    one, _, rank = block_ranks(peers, blocks, lists_ref)
    place = jnp.sum(one * (rank[:, :1] - 1.0), axis=0, keepdims=True)
    slot = (lists_ref[2:3, :] * CAP).astype(f32) + place
    mine = (lax.broadcasted_iota(i32, (blocks, entries), 0) == lists_ref[0:1, :]).astype(f32)
    earlier = lax.broadcasted_iota(i32, (entries, entries), 0) < lax.broadcasted_iota(
        i32, (entries, entries), 1
    )
    seen = jnp.dot(
        mine.astype(bf16), jnp.where(earlier, 1.0, 0.0).astype(bf16), preferred_element_type=f32
    )
    turn = jnp.sum(mine * seen, axis=0, keepdims=True).astype(i32)
    count = jnp.sum(mine, axis=1, keepdims=True).astype(i32)
    groups = (count + QUAD - 1) // QUAD
    above = lax.broadcasted_iota(i32, (blocks, blocks), 1) < lax.broadcasted_iota(
        i32, (blocks, blocks), 0
    )
    base = jnp.dot(
        jnp.where(above, 1.0, 0.0).astype(bf16),
        jnp.broadcast_to(groups.astype(f32), (blocks, 128)).astype(bf16),
        preferred_element_type=f32,
    )[:, :1]
    start = jnp.sum(mine * base, axis=0, keepdims=True).astype(i32)
    goal = (start + turn // QUAD) * QUAD + turn % QUAD
    found = (lax.broadcasted_iota(i32, (places, entries), 0) == goal).astype(f32).astype(bf16)
    number = lax.broadcasted_iota(i32, (1, entries), 1).astype(f32)
    facts = jnp.concatenate(
        [number, slot, jnp.ones((1, entries), f32), jnp.zeros((5, entries), f32)], axis=0
    )
    table = lax.dot_general(
        facts.astype(bf16), found, (((1,), (1,)), ((), ())), preferred_element_type=f32
    )
    order_ref[...] = table[0:1, :].astype(i32)
    slot_ref[...] = jnp.where(table[2:3, :] > 0.5, table[1:2, :], float(peers * CAP)).astype(i32)
    quad = lax.broadcasted_iota(i32, (blocks, quads), 1).astype(f32)
    inside = (quad >= base) & (quad < base + groups.astype(f32))
    name = lax.broadcasted_iota(i32, (blocks, quads), 0)
    row_ref[...] = jnp.sum(jnp.where(inside, name.astype(f32), 0.0), axis=0, keepdims=True).astype(i32)


def signs(node, first, second):
    one = jnp.ones(node.shape, bf16)
    return jnp.where(node == first, one, jnp.where(node == second, -one, jnp.zeros_like(one)))


def charges(ends_ref, zb_ref, start, chunk):
    blocks, size, width = zb_ref.shape
    branches = blocks * size
    node = lax.broadcasted_iota(i32, (16, branches), 0).astype(i16)
    groups = []
    for g in range(chunk // 16):
        row = node + jnp.full((16, branches), start + 16 * g, i32).astype(i16)
        groups.append(signs(row, ends_ref[:16, :], ends_ref[16:, :]))
    return jnp.dot(
        jnp.concatenate(groups, axis=0),
        zb_ref[...].reshape(branches, width),
        preferred_element_type=f32,
    ).astype(bf16)


def emit(
    plan, w_of, ends_ref, jacobi_ref, needs_ref, place_ref, table_ref, rows_ref,
    z_ref, zb_out_ref, right_ref, left_ref, zv_ref, zb_ref, both_ref, sems,
):
    blocks, size, width = zb_ref.shape
    peers = needs_ref.shape[0]
    base = plan[0]
    node_rows = rows_ref.shape[0]
    nodes = right_ref.shape[0] - (plan[1] - base) * size - node_rows
    for n in range(blocks):
        z = jnp.dot(table_ref[jacobi_ref[n]], w_of(n).astype(bf16), preferred_element_type=f32)
        zv_ref[n] = z
        zb_ref[n] = z.astype(bf16)
    pack = pltpu.make_async_copy(zb_ref, zb_out_ref, sems.at[1])
    pack.start()
    save = pltpu.make_async_copy(zv_ref, z_ref, sems.at[0])
    save.start()
    mine = place_ref[0]
    left_ref[pl.ds(nodes, node_rows), :] = rows_ref[...]
    right_ref[pl.ds(nodes, node_rows), :] = rows_ref[...]
    for s in range(base, plan[1]):
        for out, step in ((right_ref, 1), (left_ref, -1)):
            peer = jnp.clip(mine + step, 0, peers - 1)
            there = nodes + node_rows + (s - base) * size
            out[pl.ds(there, size), :] = zb_ref[needs_ref[peer, s]]
    chunk = nodes if base < CAP else 128

    def body(step, carry):
        start = pl.multiple_of(step * chunk, chunk)
        both_ref[pl.ds(start, chunk), :] = charges(ends_ref, zb_ref, start, chunk)
        return carry

    lax.fori_loop(0, 2 * nodes // chunk, body, 0)
    left_ref[pl.ds(0, nodes), :] = both_ref[pl.ds(0, nodes), :]
    right_ref[pl.ds(0, nodes), :] = both_ref[pl.ds(nodes, nodes), :]
    save.wait()
    pack.wait()


def pack_kernel(plan, needs_ref, place_ref, zb_ref, send_ref, own_ref, *extra_refs):
    peers, base = send_ref.shape[:2]
    mine = place_ref[0]
    for j in range(peers):
        for s in range(base):
            send_ref[j, s] = zb_ref[needs_ref[j, s]]
    for s in range(CAP):
        own_ref[s] = zb_ref[needs_ref[mine, s]]
    at = 0
    for distance in range(2, peers):
        if plan[distance] > base:
            for step in (distance, -distance):
                peer = jnp.clip(mine + step, 0, peers - 1)
                for s in range(base, plan[distance]):
                    extra_refs[at][s - base] = zb_ref[needs_ref[peer, s]]
                at += 1


def start_kernel(
    plan, pay_ref, side_ref, ends_ref, jacobi_ref, needs_ref, place_ref, table_ref, rows_ref,
    w_ref, beta_ref, z_ref, zb_out_ref, right_ref, left_ref, zv_ref, zb_ref, both_ref, sems,
):
    total = jnp.sum(pay_ref[:, 0, :], axis=0, keepdims=True)
    beta = jnp.sqrt(both_parts(total))
    beta_ref[...] = jnp.broadcast_to(beta, beta_ref.shape)
    w_ref[...] = side_ref[...] / beta[None]
    emit(
        plan, lambda n: w_ref[n], ends_ref, jacobi_ref, needs_ref, place_ref, table_ref, rows_ref,
        z_ref, zb_out_ref, right_ref, left_ref, zv_ref, zb_ref, both_ref, sems,
    )


def local_kernel(z_ref, self_ref, res_ref, freq_ref, part_ref):
    freq = freq_ref[...]
    for n in range(z_ref.shape[0]):
        z = z_ref[n]
        flux = jnp.dot(self_ref[n], z.astype(bf16), preferred_element_type=f32)
        part_ref[n] = freq * flux - turned(res_ref[n] * z)


def charge_kernel(rows_ref, left_ref, right_ref, arrived_ref, beyond_ref, charge_ref, plus_ref):
    node_rows = rows_ref.shape[0]
    nodes = NODE_ROW * node_rows // PAD
    charge_ref[:nodes] = (left_ref[...].astype(f32) + arrived_ref[:nodes].astype(f32)).astype(bf16)
    charge_ref[nodes:] = (right_ref[...].astype(f32) + beyond_ref[:nodes].astype(f32)).astype(bf16)
    own = rows_ref[...].astype(f32)
    next_rows = beyond_ref[pl.ds(nodes, node_rows), :].astype(f32)
    lanes = [own[i : i + 1, :] for i in range(nodes // NODE_ROW)]
    lanes += [next_rows[i : i + 1, :] for i in range(nodes // NODE_ROW)]
    row = jnp.concatenate(lanes, axis=1)
    plus_ref[...] = jnp.broadcast_to(row, (16, 2 * nodes)).astype(bf16)


def drop_into(acc_ref, group, freq_ref, cols_ref, charge_ref, plus_ref):
    blocks, size, width = acc_ref.shape
    scale = 1.0 / (freq_ref[...] * freq_ref[...])

    def body(step, carry):
        start = pl.multiple_of(step * group * size, group * size)
        plus = plus_ref[...]
        node = lax.broadcasted_iota(i32, plus.shape, 1).astype(i16)
        none = jnp.zeros_like(plus)
        rows = []
        for g in range(group * size // 16):
            ends = cols_ref[pl.ds(start + 16 * g, 16), :]
            rows.append(
                jnp.where(node == ends[:, 0:1], plus, jnp.where(node == ends[:, 1:2], -plus, none))
            )
        drop = jnp.dot(jnp.concatenate(rows, axis=0), charge_ref[...], preferred_element_type=f32)
        acc_ref[pl.ds(step * group, group)] = -(drop * scale).reshape(group, size, width)
        return carry

    lax.fori_loop(0, blocks // group, body, 0)


def couple(
    plan, order_ref, row_ref, slot_ref, place_ref, blocks_ref, incoming_ref, own_ref, arrived_ref,
    beyond_ref, extra_refs, drop_refs, acc_ref, source_ref, held_ref, sems, later,
):
    places = held_ref.shape[0]
    piece = RUN * QUAD
    runs = places // piece

    def copy(step):
        here = pl.ds(step * piece, piece)
        source = held_ref if order_ref is not None else blocks_ref
        return pltpu.make_async_copy(source.at[here], held_ref.at[here], sems.at[step])

    for step in range(runs):
        if order_ref is None:
            copy(step).start()
            continue

        def fetch(i, carry, step=step):
            p = step * piece + i
            pltpu.make_async_copy(
                blocks_ref.at[order_ref[0, p]], held_ref.at[p], sems.at[step]
            ).start()
            return carry

        lax.fori_loop(0, piece, fetch, 0, unroll=4)
    for fetched in later:
        fetched.start()
    peers, base, size, width = incoming_ref.shape
    extra = plan[1] - base
    head = arrived_ref.shape[0] - extra * size
    mine = place_ref[0]
    for j in range(peers):
        for s in range(base):
            source_ref[j * CAP + s] = incoming_ref[j, s]
    source_ref[peers * CAP] = jnp.zeros((size, width), bf16)
    for s in range(base, CAP):
        source_ref[mine * CAP + s] = own_ref[s]
    for distance in range(1, peers):
        for s in range(base, plan[distance]):
            for side in range(2):
                peer = mine + (-distance if side == 0 else distance)
                there = (peer >= 0) & (peer < peers)
                slot = jnp.where(there, peer * CAP + s, peers * CAP + 1)
                if distance == 1:
                    source = arrived_ref if side == 0 else beyond_ref
                    block = source[pl.ds(head + (s - base) * size, size), :]
                else:
                    block = extra_refs[2 * (distance - 2) + side][s - base]
                source_ref[slot] = block
    drop_into(acc_ref, acc_ref.shape[0] // 2 if base < CAP else 1, *drop_refs)

    def body(step, carry):
        copy(step).wait()
        for u in range(RUN):
            quad = step * RUN + u
            left = jnp.concatenate([held_ref[quad * QUAD + i] for i in range(QUAD)], axis=1)
            right = jnp.concatenate(
                [source_ref[slot_ref[0, quad * QUAD + i]] for i in range(QUAD)], axis=0
            )
            acc_ref[row_ref[0, quad]] += jnp.dot(left, right, preferred_element_type=f32)
        return carry

    lax.fori_loop(0, runs, body, 0)
    for fetched in later:
        fetched.wait()


def image_of(part_ref, freq_ref, acc_ref, n):
    return STEP * turned(part_ref[n] + freq_ref[...] * acc_ref[n])


def split(plan, rest):
    count = extras(plan)
    return rest[:count], rest[count:]


def extras(plan):
    return 2 * sum(1 for slots in plan[2:] if slots > plan[0])


def middle_kernel(
    plan, first, row_ref, slot_ref, place_ref, blocks_ref, incoming_ref, own_ref, arrived_ref,
    beyond_ref, *rest,
):
    come, rest = split(plan, rest)
    part_ref, freq_ref, cols_ref, charge_ref, plus_ref = rest[:5]
    ends_ref, jacobi_ref, needs_ref, table_ref, rows_ref = rest[5:10]
    rest = rest[10:]
    order_ref = None
    if first:
        order_ref, rest = rest[0], rest[1:]
    w_ref, z_ref, zb_out_ref, right_ref, left_ref = rest[:5]
    rest = rest[5:]
    if first:
        sorted_ref, rest = rest[0], rest[1:]
    acc_ref, source_ref, held_ref, run_sems, wv_ref, zv_ref, zb_ref, both_ref, sems = rest
    bring = pltpu.make_async_copy(part_ref, zv_ref, sems.at[0])
    couple(
        plan, order_ref, row_ref, slot_ref, place_ref, blocks_ref, incoming_ref, own_ref,
        arrived_ref, beyond_ref, come, (freq_ref, cols_ref, charge_ref, plus_ref), acc_ref,
        source_ref, held_ref, run_sems, [bring],
    )
    if first:
        keep = pltpu.make_async_copy(held_ref, sorted_ref, sems.at[3])
        keep.start()
    for n in range(wv_ref.shape[0]):
        wv_ref[n] = image_of(zv_ref, freq_ref, acc_ref, n)
    save = pltpu.make_async_copy(wv_ref, w_ref, sems.at[2])
    save.start()
    emit(
        plan, lambda n: wv_ref[n], ends_ref, jacobi_ref, needs_ref, place_ref, table_ref, rows_ref,
        z_ref, zb_out_ref, right_ref, left_ref, zv_ref, zb_ref, both_ref, sems,
    )
    save.wait()
    if first:
        keep.wait()


PAIRS = [(i, j) for j in range(ITERS + 1) for i in range(j + 1)]


def last_kernel(
    plan, row_ref, slot_ref, place_ref, blocks_ref, incoming_ref, own_ref, arrived_ref,
    beyond_ref, *rest,
):
    come, rest = split(plan, rest)
    part_ref, freq_ref, cols_ref, charge_ref, plus_ref = rest[:5]
    w0_ref, w1_ref, w2_ref, pay_ref = rest[5:9]
    acc_ref, source_ref, held_ref, run_sems, store_ref, sems = rest[9:]
    bring = [
        pltpu.make_async_copy(source, store_ref.at[at], sems.at[at])
        for at, source in enumerate((part_ref, w0_ref, w1_ref, w2_ref))
    ]
    couple(
        plan, None, row_ref, slot_ref, place_ref, blocks_ref, incoming_ref, own_ref,
        arrived_ref, beyond_ref, come, (freq_ref, cols_ref, charge_ref, plus_ref), acc_ref,
        source_ref, held_ref, run_sems, bring,
    )
    blocks = acc_ref.shape[0]

    def body(n, sums):
        w = [store_ref[1 + k, n] for k in range(ITERS)]
        w.append(image_of(store_ref.at[0], freq_ref, acc_ref, n))
        fresh = []
        for at, (i, j) in enumerate(PAIRS):
            product = (w[i] * w[j]).reshape(-1, 8, 128)
            fresh.append(sums[at] + jnp.sum(product, axis=0))
        return tuple(fresh)

    sums = lax.fori_loop(0, blocks, body, tuple(jnp.zeros((8, 128), f32) for _ in PAIRS))
    rows = [jnp.sum(s, axis=0, keepdims=True) for s in sums]
    rows = [both_parts(row) for row in rows]
    real = lane_is_real((1, 128))
    rows = [jnp.where(real, rows[k], rows[k + 1]) for k in range(0, len(rows), 2)]
    rows.append(jnp.zeros((8 - len(rows), 128), f32))
    pay_ref[...] = jnp.broadcast_to(jnp.concatenate(rows, axis=0)[None], pay_ref.shape)


def finish_kernel(pay_ref, beta_ref, z0_ref, z1_ref, z2_ref, out_ref, norm_ref):
    total = jnp.sum(pay_ref[...], axis=0)
    real = lane_is_real(total.shape)
    even = jnp.where(real, total, pltpu.roll(total, F, 1))
    odd = jnp.where(real, pltpu.roll(total, 128 - F, 1), total)
    gram = {}
    for at, (i, j) in enumerate(PAIRS):
        half = at // 2
        gram[i, j] = gram[j, i] = (odd if at % 2 else even)[half : half + 1, :]
    order = list(range(1, ITERS + 1)) + [0]
    low = {}
    for i in range(ITERS + 1):
        for j in range(i + 1):
            value = gram[order[i], order[j]]
            for k in range(j):
                value = value - low[i, k] * low[j, k]
            low[i, j] = jnp.sqrt(jnp.maximum(value, 0.0)) if i == j else value / low[j, j]
    weights = [None] * ITERS
    for i in reversed(range(ITERS)):
        value = low[ITERS, i]
        for k in range(i + 1, ITERS):
            value = value - low[k, i] * weights[k]
        weights[i] = value / low[i, i]
    beta = beta_ref[0:1, :]
    norm = low[ITERS, ITERS] * beta
    norm_ref[...] = jnp.concatenate([norm, pltpu.roll(norm, 2 * F, 1)], axis=0)[:, :F]
    weights = [STEP * beta * weight for weight in weights]
    for n in range(out_ref.shape[0]):
        out_ref[n] = weights[0] * z0_ref[n] + weights[1] * z1_ref[n] + weights[2] * z2_ref[n]


def call(kernel, outs, ins, places=None, **more):
    return pl.pallas_call(
        kernel,
        out_shape=outs,
        in_specs=ins,
        out_specs=places or [VM] * len(outs),
        compiler_params=pltpu.CompilerParams(vmem_limit_bytes=LIMIT),
        **more,
    )


def iterate(
    plan, pay, right_side, jacobi_ids, needs, place, table, ends, ends_col, selfs, res, scale,
    freq, tables, couple_blocks,
):
    order, slots, rows = tables
    peers = needs.shape[0]
    devices = pay.shape[0]
    blocks, size, width = right_side.shape
    nodes = NODE_ROW * scale.shape[0] // PAD
    base = plan[0]
    far = [d for d in range(2, peers) if plan[d] > base]
    halo = kept((nodes + scale.shape[0] + (plan[1] - base) * size, width), bf16)
    vec = kept((blocks, size, width), f32)
    emitted = [vec, kept((blocks, size, width), bf16), halo, halo]
    packed = [
        kept((peers, base, size, width), bf16),
        kept((CAP, size, width), bf16),
    ] + [kept((plan[d] - base, size, width), bf16) for d in far for side in range(2)]
    spots = [HB, HB, VM, VM]
    buffers = [
        pltpu.VMEM((blocks, size, width), f32),
        pltpu.VMEM((blocks, size, width), bf16),
        pltpu.VMEM((2 * nodes, width), bf16),
        pltpu.SemaphoreType.DMA((4,)),
    ]
    places = order.shape[1]
    coupling = [
        pltpu.VMEM((blocks, size, width), f32),
        pltpu.VMEM((peers * CAP + 2, size, width), bf16),
        pltpu.VMEM((places, size, size), bf16),
        pltpu.SemaphoreType.DMA((places // (RUN * QUAD),)),
    ]
    w, beta, z, zb, right, left = call(
        functools.partial(start_kernel, plan),
        [vec, whole((8, width), f32)] + emitted,
        [VM, VM, VM, SM, SM, SM, VM, VM],
        [VM, VM] + spots,
        scratch_shapes=buffers,
    )(near_core(pay), right_side, ends, jacobi_ids, needs, place, table, scale)
    basis = [w]
    fields = [z]
    for step in range(ITERS):

        def moved(value, distance):
            route = [(i, i + distance) for i in range(peers) if 0 <= i + distance < peers]
            return near_core(lax.ppermute(value, "narrow", route))

        arrived = moved(right, 1)
        beyond = moved(left, -1)
        send, own, *go = call(functools.partial(pack_kernel, plan), packed, [SM, SM, VM])(
            needs, place, in_hbm(zb)
        )
        come = []
        for at, d in enumerate(far):
            come += [moved(go[2 * at], d), moved(go[2 * at + 1], -d)]
        incoming = near_core(lax.all_to_all(send, "narrow", 0, 0))
        later, send = lax.optimization_barrier((z, send))
        (part,) = call(local_kernel, [vec], [VM] * 4)(in_hbm(later), selfs, res, freq)
        head = pl.BlockSpec((nodes, width), lambda i: (0, 0))
        charge, plus = call(
            charge_kernel,
            [kept((2 * nodes, width), bf16), kept((16, 2 * nodes), bf16)],
            [VM, head, head, VM, VM],
            grid=(1,),
            cost_estimate=pl.CostEstimate(
                flops=WEIGHT * blocks * size * nodes * width,
                bytes_accessed=WEIGHT * blocks * size * width,
                transcendentals=0,
            ),
        )(scale, in_hbm(left), in_hbm(right), arrived, beyond)
        first = step == 0
        held = couple_blocks if first else sorted_blocks
        common = (
            rows, slots, place, in_hbm(held), incoming, in_hbm(own), arrived, beyond, *come,
            in_hbm(part), freq, ends_col, in_hbm(charge), in_hbm(plus),
        )
        specs = [SM, SM, SM, HB] + [VM] * (4 + len(come)) + [HB] + [VM] * 4
        if step + 1 < ITERS:
            w, z, zb, right, left, *copies = call(
                functools.partial(middle_kernel, plan, first),
                [vec] + emitted + ([kept((places, size, size), bf16)] if first else []),
                specs + [VM, SM, SM, VM, VM] + ([SM] if first else []),
                [HB] + spots + ([HB] if first else []),
                scratch_shapes=coupling + [pltpu.VMEM((blocks, size, width), f32)] + buffers,
            )(*common, ends, jacobi_ids, needs, table, scale, *([order] if first else []))
            if first:
                (sorted_blocks,) = copies
            basis.append(w)
            fields.append(z)
        else:
            (sums,) = call(
                functools.partial(last_kernel, plan),
                [whole((devices, 8, 128), f32)],
                specs + [HB] * 3,
                scratch_shapes=coupling
                + [
                    pltpu.VMEM((ITERS + 1, blocks, size, width), f32),
                    pltpu.SemaphoreType.DMA((ITERS + 1,)),
                ],
            )(*common, *map(in_hbm, basis))
    sums = near_core(lax.all_to_all(sums, AXES, 0, 0))
    return call(finish_kernel, [vec, whole((CASES, F), f32)], [VM] * 5)(
        sums, beta, *map(in_hbm, fields)
    )


def on_device(
    right_side, resistance, omega, pcoef, branch_nodes, self_blocks, couple_list, couple_blocks,
    jacobi_ids, preconditioners,
):
    blocks, size, width = right_side.shape
    nodes = pcoef.shape[0]
    entries = couple_list.shape[1]
    peers = lax.axis_size("narrow")
    devices = peers * lax.axis_size("wide")
    group = lax.axis_index("wide")
    mine = lax.axis_index("narrow")
    node_rows = nodes // NODE_ROW
    freq = jnp.tile(omega, 2 * CASES).reshape(1, width)
    pairs = jnp.transpose(branch_nodes, (1, 0, 2)).reshape(2, blocks * size)
    pairs = jnp.where(pairs[0] == pairs[1], -1, pairs)
    ends = jnp.repeat(pairs.astype(i16), 16, axis=0)
    ends_col = jnp.transpose(pairs).astype(i16)
    quads = (entries + (QUAD - 1) * blocks) // QUAD
    quads = -(-quads // RUN) * RUN

    (pay,) = call(
        functools.partial(setup_kernel, peers, blocks),
        [whole((devices, 8, 128), f32)],
        [VM] * 2,
    )(in_hbm(couple_list), in_hbm(right_side))
    pay = lax.all_to_all(pay, AXES, 0, 0)
    order, slots, rows = call(
        functools.partial(order_kernel, peers, blocks),
        [whole((1, quads * QUAD), i32), whole((1, quads * QUAD), i32), whole((1, quads), i32)],
        [VM],
    )(couple_list)
    needs = lax.dynamic_slice(
        pay, (group * peers, 1, mine * CAP), (peers, 1, CAP)
    ).reshape(peers, CAP).astype(i32)
    rows16 = jnp.pad(pcoef.astype(bf16).reshape(node_rows, 128), ((0, node_rows), (0, 0)))
    shared = (
        pay, in_hbm(right_side), jacobi_ids, needs, mine.reshape(1), in_hbm(preconditioners),
        in_hbm(ends), in_hbm(ends_col), in_hbm(self_blocks),
        in_hbm(resistance.reshape(blocks, size, 1)), in_hbm(rows16), freq, (order, slots, rows),
        in_hbm(couple_blocks),
    )
    full = (CAP,) * peers
    near = (2,) + tuple(max(2, CAP // distance) for distance in range(1, peers))
    reach = np.abs(np.arange(devices)[:, None] % peers - np.arange(peers)[None, :])
    allowed = np.where(reach == 0, CAP, np.asarray(near)[reach]).astype(np.float32)
    fits = jnp.all(pay[:, 2, :peers] <= allowed)
    return lax.cond(
        fits, lambda given: iterate(near, *given), lambda given: iterate(full, *given), shared
    )


def solution(mesh):
    placed = (
        P(AXES, None, None),
        P(AXES, None),
        P(),
        P(AXES),
        P(AXES, None, None),
        P(AXES, None, None),
        P(None, AXES),
        P(AXES, None, None),
        P(AXES),
        P(),
    )
    return jax.shard_map(
        on_device,
        mesh=mesh,
        in_specs=placed,
        out_specs=(P(AXES, None, None), P()),
        check_vma=False,
    )
```

```python
import functools
import jax
import jax.numpy as jnp
import numpy as np
from jax import lax
from jax.experimental import pallas as pl
from jax.experimental.pallas import tpu as pltpu
from jax.sharding import PartitionSpec as P

F = 32
CASES = 2
ITERS = 3
CAP = 4
AXES = ("wide", "narrow")
STEP = 2.0**-8
LIMIT = 40 * 1024 * 1024
QUAD = 4
RUN = 17
WEIGHT = 64
NODE_ROW = 128
PAD = 2
f32 = jnp.float32
bf16 = jnp.bfloat16
i32 = jnp.int32
i16 = jnp.int16


def whole(shape, dtype):
    return jax.ShapeDtypeStruct(shape, dtype)


def kept(shape, dtype):
    return pltpu.HBM(shape, dtype)


def in_hbm(value):
    return pltpu.with_memory_space_constraint(value, pltpu.HBM)


def near_core(value):
    return pltpu.with_memory_space_constraint(value, pltpu.VMEM)


VM = pl.BlockSpec(memory_space=pltpu.VMEM)
SM = pl.BlockSpec(memory_space=pltpu.SMEM)
HB = pl.BlockSpec(memory_space=pl.ANY)


def lane_is_real(shape):
    lane = lax.broadcasted_iota(i32, shape, len(shape) - 1)
    return lax.rem(lane, 2 * F) < F


def both_parts(row):
    other = jnp.where(lane_is_real(row.shape), pltpu.roll(row, 128 - F, 1), pltpu.roll(row, F, 1))
    return row + other


def turned(values):
    return jnp.where(
        lane_is_real(values.shape),
        -pltpu.roll(values, 128 - F, 1),
        pltpu.roll(values, F, 1),
    )


def block_ranks(peers, blocks, lists_ref):
    keys = peers * blocks
    entries = lists_ref.shape[1]
    key = lists_ref[2:3, :] * blocks + lists_ref[1:2, :]
    one = (lax.broadcasted_iota(i32, (keys, entries), 0) == key).astype(f32)
    present = jnp.max(one, axis=1, keepdims=True)
    row = lax.broadcasted_iota(i32, (keys, keys), 0)
    col = lax.broadcasted_iota(i32, (keys, keys), 1)
    before = jnp.where((row // blocks == col // blocks) & (col <= row), 1.0, 0.0).astype(bf16)
    rank = jnp.dot(
        before,
        jnp.broadcast_to(present, (keys, 128)).astype(bf16),
        preferred_element_type=f32,
    )
    return one, present, rank


def setup_kernel(peers, blocks, lists_ref, right_ref, pay_ref):
    keys = peers * blocks
    _, present, rank = block_ranks(peers, blocks, lists_ref)
    lane = lax.broadcasted_iota(i32, (keys, 128), 1)
    name = lax.broadcasted_iota(i32, (keys, 128), 0)
    chosen = (
        (name // blocks == lane // CAP)
        & (rank == (lane % CAP + 1).astype(f32))
        & (present > 0.0)
    )
    needs = jnp.sum(jnp.where(chosen, (name % blocks).astype(f32), 0.0), axis=0, keepdims=True)
    held = jnp.sum(jnp.where(name // blocks == lane, present, 0.0), axis=0, keepdims=True)
    right = right_ref[...]
    squares = jnp.sum(jnp.sum(right * right, axis=0), axis=0, keepdims=True)
    rows = jnp.concatenate([squares, needs, held, jnp.zeros((5, 128), f32)], axis=0)
    pay_ref[...] = jnp.broadcast_to(rows[None], pay_ref.shape)


def order_kernel(
    peers, blocks, lists_ref, pairs_ref, pcoef_ref, omega_ref, order_ref, slot_ref, row_ref, ends_ref,
    rows_ref, cols_ref, freq_ref,
):
    for k in range(2):
        row = jnp.broadcast_to(pairs_ref[k : k + 1, :], (16, pairs_ref.shape[1]))
        ends_ref[16 * k : 16 * (k + 1), :] = row.astype(i16)
    numbers = pairs_ref[...].astype(f32)
    numbers = jnp.concatenate([numbers, jnp.zeros((6, numbers.shape[1]), f32)], axis=0)
    cols_ref[...] = jnp.transpose(numbers)[:, :2].astype(i32).astype(i16)
    freq_ref[...] = jnp.concatenate([omega_ref[...]] * (2 * CASES), axis=1)
    own = pcoef_ref[...]
    rows_ref[...] = jnp.concatenate([own, jnp.zeros_like(own)], axis=0).astype(bf16)
    entries = lists_ref.shape[1]
    places = order_ref.shape[1]
    quads = row_ref.shape[1]
    one, _, rank = block_ranks(peers, blocks, lists_ref)
    place = jnp.sum(one * (rank[:, :1] - 1.0), axis=0, keepdims=True)
    slot = (lists_ref[2:3, :] * CAP).astype(f32) + place
    mine = (lax.broadcasted_iota(i32, (blocks, entries), 0) == lists_ref[0:1, :]).astype(f32)
    earlier = lax.broadcasted_iota(i32, (entries, entries), 0) < lax.broadcasted_iota(
        i32, (entries, entries), 1
    )
    seen = jnp.dot(
        mine.astype(bf16), jnp.where(earlier, 1.0, 0.0).astype(bf16), preferred_element_type=f32
    )
    turn = jnp.sum(mine * seen, axis=0, keepdims=True).astype(i32)
    count = jnp.sum(mine, axis=1, keepdims=True).astype(i32)
    groups = (count + QUAD - 1) // QUAD
    above = lax.broadcasted_iota(i32, (blocks, blocks), 1) < lax.broadcasted_iota(
        i32, (blocks, blocks), 0
    )
    base = jnp.dot(
        jnp.where(above, 1.0, 0.0).astype(bf16),
        jnp.broadcast_to(groups.astype(f32), (blocks, 128)).astype(bf16),
        preferred_element_type=f32,
    )[:, :1]
    start = jnp.sum(mine * base, axis=0, keepdims=True).astype(i32)
    goal = (start + turn // QUAD) * QUAD + turn % QUAD
    found = (lax.broadcasted_iota(i32, (places, entries), 0) == goal).astype(f32).astype(bf16)
    number = lax.broadcasted_iota(i32, (1, entries), 1).astype(f32)
    facts = jnp.concatenate(
        [number, slot, jnp.ones((1, entries), f32), jnp.zeros((5, entries), f32)], axis=0
    )
    table = lax.dot_general(
        facts.astype(bf16), found, (((1,), (1,)), ((), ())), preferred_element_type=f32
    )
    order_ref[...] = table[0:1, :].astype(i32)
    slot_ref[...] = jnp.where(table[2:3, :] > 0.5, table[1:2, :], float(peers * CAP)).astype(i32)
    quad = lax.broadcasted_iota(i32, (blocks, quads), 1).astype(f32)
    inside = (quad >= base) & (quad < base + groups.astype(f32))
    name = lax.broadcasted_iota(i32, (blocks, quads), 0)
    row_ref[...] = jnp.sum(jnp.where(inside, name.astype(f32), 0.0), axis=0, keepdims=True).astype(i32)


def signs(node, first, second):
    one = jnp.ones(node.shape, bf16)
    return jnp.where(node == first, one, jnp.where(node == second, -one, jnp.zeros_like(one)))


def charges(ends_ref, zb_ref, start, chunk):
    blocks, size, width = zb_ref.shape
    branches = blocks * size
    node = lax.broadcasted_iota(i32, (16, branches), 0).astype(i16)
    groups = []
    for g in range(chunk // 16):
        row = node + jnp.full((16, branches), start + 16 * g, i32).astype(i16)
        groups.append(signs(row, ends_ref[:16, :], ends_ref[16:, :]))
    return jnp.dot(
        jnp.concatenate(groups, axis=0),
        zb_ref[...].reshape(branches, width),
        preferred_element_type=f32,
    ).astype(bf16)


def emit(
    plan, w_of, ends_ref, jacobi_ref, needs_ref, place_ref, table_ref, rows_ref,
    z_ref, send_ref, own_ref, right_ref, left_ref, go_refs, zv_ref, zb_ref, sv_ref, both_ref, sems,
):
    blocks, size, width = zb_ref.shape
    peers = needs_ref.shape[0]
    base = plan[0]
    node_rows = rows_ref.shape[0]
    nodes = right_ref.shape[0] - (plan[1] - base) * size - node_rows
    for n in range(blocks):
        z = jnp.dot(table_ref[jacobi_ref[n]], w_of(n).astype(bf16), preferred_element_type=f32)
        zv_ref[n] = z
        zb_ref[n] = z.astype(bf16)
    for j in range(peers):
        for s in range(base):
            sv_ref[j, s] = zb_ref[needs_ref[j, s]]
    pack = pltpu.make_async_copy(sv_ref, send_ref, sems.at[1])
    pack.start()
    save = pltpu.make_async_copy(zv_ref, z_ref, sems.at[0])
    save.start()
    mine = place_ref[0]
    for s in range(CAP):
        own_ref[s] = zb_ref[needs_ref[mine, s]]
    left_ref[pl.ds(nodes, node_rows), :] = rows_ref[...]
    right_ref[pl.ds(nodes, node_rows), :] = rows_ref[...]
    for s in range(base, plan[1]):
        for out, step in ((right_ref, 1), (left_ref, -1)):
            peer = jnp.clip(mine + step, 0, peers - 1)
            there = nodes + node_rows + (s - base) * size
            out[pl.ds(there, size), :] = zb_ref[needs_ref[peer, s]]
    at = 0
    for distance in range(2, peers):
        if plan[distance] > base:
            for step in (distance, -distance):
                peer = jnp.clip(mine + step, 0, peers - 1)
                for s in range(base, plan[distance]):
                    go_refs[at][s - base] = zb_ref[needs_ref[peer, s]]
                at += 1
    chunk = nodes if base < CAP else 128

    def body(step, carry):
        start = pl.multiple_of(step * chunk, chunk)
        both_ref[pl.ds(start, chunk), :] = charges(ends_ref, zb_ref, start, chunk)
        return carry

    lax.fori_loop(0, 2 * nodes // chunk, body, 0)
    left_ref[pl.ds(0, nodes), :] = both_ref[pl.ds(0, nodes), :]
    right_ref[pl.ds(0, nodes), :] = both_ref[pl.ds(nodes, nodes), :]
    save.wait()
    pack.wait()


def start_kernel(
    plan, pay_ref, side_ref, ends_ref, jacobi_ref, needs_ref, place_ref, table_ref, rows_ref,
    w_ref, beta_ref, z_ref, send_ref, own_ref, right_ref, left_ref, *rest,
):
    go, rest = split(plan, rest)
    wv_ref, zv_ref, zb_ref, sv_ref, both_ref, sems = rest
    total = jnp.sum(pay_ref[:, 0, :], axis=0, keepdims=True)
    beta = jnp.sqrt(both_parts(total))
    beta_ref[...] = jnp.broadcast_to(beta, beta_ref.shape)
    wv_ref[...] = side_ref[...] / beta[None]
    save = pltpu.make_async_copy(wv_ref, w_ref, sems.at[2])
    save.start()
    emit(
        plan, lambda n: wv_ref[n], ends_ref, jacobi_ref, needs_ref, place_ref, table_ref, rows_ref,
        z_ref, send_ref, own_ref, right_ref, left_ref, go, zv_ref, zb_ref, sv_ref, both_ref, sems,
    )
    save.wait()


def local_kernel(z_ref, self_ref, res_ref, freq_ref, part_ref):
    freq = freq_ref[...]
    res = jnp.transpose(res_ref[...])
    for n in range(z_ref.shape[0]):
        z = z_ref[n]
        flux = jnp.dot(self_ref[n], z.astype(bf16), preferred_element_type=f32)
        part_ref[n] = freq * flux - turned(res[:, n : n + 1] * z)


def charge_kernel(rows_ref, left_ref, right_ref, arrived_ref, beyond_ref, charge_ref, plus_ref):
    node_rows = rows_ref.shape[0]
    nodes = NODE_ROW * node_rows // PAD
    charge_ref[:nodes] = (left_ref[...].astype(f32) + arrived_ref[:nodes].astype(f32)).astype(bf16)
    charge_ref[nodes:] = (right_ref[...].astype(f32) + beyond_ref[:nodes].astype(f32)).astype(bf16)
    own = rows_ref[...].astype(f32)
    next_rows = beyond_ref[pl.ds(nodes, node_rows), :].astype(f32)
    lanes = [own[i : i + 1, :] for i in range(nodes // NODE_ROW)]
    lanes += [next_rows[i : i + 1, :] for i in range(nodes // NODE_ROW)]
    row = jnp.concatenate(lanes, axis=1)
    plus_ref[...] = jnp.broadcast_to(row, (16, 2 * nodes)).astype(bf16)


def drop_into(acc_ref, group, beside, freq_ref, cols_ref, charge_ref, plus_ref):
    blocks, size, width = acc_ref.shape
    scale = 1.0 / (freq_ref[...] * freq_ref[...])

    def body(step, carry):
        start = pl.multiple_of(step * group * size, group * size)
        beside(step)
        plus = plus_ref[...]
        node = lax.broadcasted_iota(i32, plus.shape, 1).astype(i16)
        none = jnp.zeros_like(plus)
        rows = []
        for g in range(group * size // 16):
            ends = cols_ref[pl.ds(start + 16 * g, 16), :]
            rows.append(
                jnp.where(node == ends[:, 0:1], plus, jnp.where(node == ends[:, 1:2], -plus, none))
            )
        drop = jnp.dot(jnp.concatenate(rows, axis=0), charge_ref[...], preferred_element_type=f32)
        acc_ref[pl.ds(step * group, group)] = -(drop * scale).reshape(group, size, width)
        return carry

    lax.fori_loop(0, blocks // group, body, 0)


def couple(
    plan, order_ref, row_ref, slot_ref, place_ref, blocks_ref, incoming_ref, own_ref, arrived_ref,
    beyond_ref, extra_refs, drop_refs, acc_ref, source_ref, held_ref, sems, later,
):
    places = held_ref.shape[0]
    piece = RUN * QUAD
    runs = places // piece

    def copy(step):
        here = pl.ds(step * piece, piece)
        source = held_ref if order_ref is not None else blocks_ref
        return pltpu.make_async_copy(source.at[here], held_ref.at[here], sems.at[step])

    def fetch(i, carry, step):
        p = step * piece + i
        pltpu.make_async_copy(
            blocks_ref.at[order_ref[0, p]], held_ref.at[p], sems.at[step]
        ).start()
        return carry

    if order_ref is None:
        for step in range(runs):
            copy(step).start()
    for fetched in later:
        fetched.start()
    peers, base, size, width = incoming_ref.shape
    extra = plan[1] - base
    head = arrived_ref.shape[0] - extra * size
    mine = place_ref[0]
    for j in range(peers):
        for s in range(base):
            source_ref[j * CAP + s] = incoming_ref[j, s]
    source_ref[peers * CAP] = jnp.zeros((size, width), bf16)
    for s in range(base, CAP):
        source_ref[mine * CAP + s] = own_ref[s]
    for distance in range(1, peers):
        for s in range(base, plan[distance]):
            for side in range(2):
                peer = mine + (-distance if side == 0 else distance)
                there = (peer >= 0) & (peer < peers)
                slot = jnp.where(there, peer * CAP + s, peers * CAP + 1)
                if distance == 1:
                    source = arrived_ref if side == 0 else beyond_ref
                    block = source[pl.ds(head + (s - base) * size, size), :]
                else:
                    block = extra_refs[2 * (distance - 2) + side][s - base]
                source_ref[slot] = block
    halves = base < CAP and runs % 2 == 0

    def beside(step):
        if order_ref is not None and halves:
            for r in range(runs // 2):
                for i in range(piece):
                    fetch(i, 0, step=step * (runs // 2) + r)

    if order_ref is not None and not halves:
        for step in range(runs):
            lax.fori_loop(0, piece, functools.partial(fetch, step=step), 0)
    drop_into(acc_ref, acc_ref.shape[0] // 2 if base < CAP else 1, beside, *drop_refs)

    def body(step, carry):
        copy(step).wait()
        for u in range(RUN):
            quad = step * RUN + u
            left = jnp.concatenate([held_ref[quad * QUAD + i] for i in range(QUAD)], axis=1)
            right = jnp.concatenate(
                [source_ref[slot_ref[0, quad * QUAD + i]] for i in range(QUAD)], axis=0
            )
            acc_ref[row_ref[0, quad]] += jnp.dot(left, right, preferred_element_type=f32)
        return carry

    lax.fori_loop(0, runs, body, 0)
    for fetched in later:
        fetched.wait()


def image_of(part_ref, freq_ref, acc_ref, n):
    return STEP * turned(part_ref[n] + freq_ref[...] * acc_ref[n])


def split(plan, rest):
    count = extras(plan)
    return rest[:count], rest[count:]


def extras(plan):
    return 2 * sum(1 for slots in plan[2:] if slots > plan[0])


def middle_kernel(
    plan, first, row_ref, slot_ref, place_ref, blocks_ref, incoming_ref, own_in_ref, arrived_ref,
    beyond_ref, *rest,
):
    come, rest = split(plan, rest)
    part_ref, freq_ref, cols_ref, charge_ref, plus_ref = rest[:5]
    ends_ref, jacobi_ref, needs_ref, table_ref, rows_ref = rest[5:10]
    rest = rest[10:]
    order_ref = None
    if first:
        order_ref, rest = rest[0], rest[1:]
    w_ref, z_ref, send_ref, own_ref, right_ref, left_ref = rest[:6]
    go, rest = split(plan, rest[6:])
    if first:
        sorted_ref, rest = rest[0], rest[1:]
    acc_ref, source_ref, held_ref, run_sems, wv_ref, zv_ref, zb_ref, sv_ref, both_ref, sems = rest
    bring = pltpu.make_async_copy(part_ref, zv_ref, sems.at[0])
    couple(
        plan, order_ref, row_ref, slot_ref, place_ref, blocks_ref, incoming_ref, own_in_ref,
        arrived_ref, beyond_ref, come, (freq_ref, cols_ref, charge_ref, plus_ref), acc_ref,
        source_ref, held_ref, run_sems, [bring],
    )
    if first:
        keep = pltpu.make_async_copy(held_ref, sorted_ref, sems.at[3])
        keep.start()
    for n in range(wv_ref.shape[0]):
        wv_ref[n] = image_of(zv_ref, freq_ref, acc_ref, n)
    save = pltpu.make_async_copy(wv_ref, w_ref, sems.at[2])
    save.start()
    emit(
        plan, lambda n: wv_ref[n], ends_ref, jacobi_ref, needs_ref, place_ref, table_ref, rows_ref,
        z_ref, send_ref, own_ref, right_ref, left_ref, go, zv_ref, zb_ref, sv_ref, both_ref, sems,
    )
    save.wait()
    if first:
        keep.wait()


PAIRS = [(i, j) for j in range(ITERS + 1) for i in range(j + 1)]


def last_kernel(
    plan, row_ref, slot_ref, place_ref, blocks_ref, incoming_ref, own_ref, arrived_ref,
    beyond_ref, *rest,
):
    come, rest = split(plan, rest)
    part_ref, freq_ref, cols_ref, charge_ref, plus_ref = rest[:5]
    w0_ref, w1_ref, w2_ref, pay_ref = rest[5:9]
    acc_ref, source_ref, held_ref, run_sems, store_ref, sems = rest[9:]
    bring = [
        pltpu.make_async_copy(source, store_ref.at[at], sems.at[at])
        for at, source in enumerate((part_ref, w0_ref, w1_ref, w2_ref))
    ]
    couple(
        plan, None, row_ref, slot_ref, place_ref, blocks_ref, incoming_ref, own_ref,
        arrived_ref, beyond_ref, come, (freq_ref, cols_ref, charge_ref, plus_ref), acc_ref,
        source_ref, held_ref, run_sems, bring,
    )
    blocks = acc_ref.shape[0]

    def body(n, sums):
        w = [store_ref[1 + k, n] for k in range(ITERS)]
        w.append(image_of(store_ref.at[0], freq_ref, acc_ref, n))
        fresh = []
        for at, (i, j) in enumerate(PAIRS):
            product = (w[i] * w[j]).reshape(-1, 8, 128)
            fresh.append(sums[at] + jnp.sum(product, axis=0))
        return tuple(fresh)

    sums = lax.fori_loop(0, blocks, body, tuple(jnp.zeros((8, 128), f32) for _ in PAIRS))
    rows = [jnp.sum(s, axis=0, keepdims=True) for s in sums]
    rows = [both_parts(row) for row in rows]
    real = lane_is_real((1, 128))
    rows = [jnp.where(real, rows[k], rows[k + 1]) for k in range(0, len(rows), 2)]
    rows.append(jnp.zeros((8 - len(rows), 128), f32))
    pay_ref[...] = jnp.broadcast_to(jnp.concatenate(rows, axis=0)[None], pay_ref.shape)


def finish_kernel(
    pay_ref, beta_ref, z0_ref, z1_ref, z2_ref, out_ref, norm_ref, held_ref, made_ref, in_sems, out_sems,
):
    parts = out_sems.shape[0]
    group = out_ref.shape[0] // parts
    arrive = []
    for p in range(parts):
        here = pl.ds(p * group, group)
        arrive.append(
            [
                pltpu.make_async_copy(z.at[here], held_ref.at[k, here], in_sems.at[p, k])
                for k, z in enumerate((z0_ref, z1_ref, z2_ref))
            ]
        )
        for copy in arrive[p]:
            copy.start()
    total = jnp.sum(pay_ref[...], axis=0)
    real = lane_is_real(total.shape)
    even = jnp.where(real, total, pltpu.roll(total, F, 1))
    odd = jnp.where(real, pltpu.roll(total, 128 - F, 1), total)
    gram = {}
    for at, (i, j) in enumerate(PAIRS):
        half = at // 2
        gram[i, j] = gram[j, i] = (odd if at % 2 else even)[half : half + 1, :]
    order = list(range(1, ITERS + 1)) + [0]
    low = {}
    for i in range(ITERS + 1):
        for j in range(i + 1):
            value = gram[order[i], order[j]]
            for k in range(j):
                value = value - low[i, k] * low[j, k]
            low[i, j] = jnp.sqrt(jnp.maximum(value, 0.0)) if i == j else value / low[j, j]
    weights = [None] * ITERS
    for i in reversed(range(ITERS)):
        value = low[ITERS, i]
        for k in range(i + 1, ITERS):
            value = value - low[k, i] * weights[k]
        weights[i] = value / low[i, i]
    beta = beta_ref[0:1, :]
    norm = low[ITERS, ITERS] * beta
    norm_ref[...] = jnp.concatenate([norm, pltpu.roll(norm, 2 * F, 1)], axis=0)[:, :F]
    weights = [STEP * beta * weight for weight in weights]
    leave = []
    for p in range(parts):
        for copy in arrive[p]:
            copy.wait()
        for n in range(p * group, (p + 1) * group):
            total = weights[0] * held_ref[0, n]
            for k in range(1, ITERS):
                total = total + weights[k] * held_ref[k, n]
            made_ref[n] = total
        here = pl.ds(p * group, group)
        leave.append(pltpu.make_async_copy(made_ref.at[here], out_ref.at[here], out_sems.at[p]))
        leave[p].start()
    for copy in leave:
        copy.wait()


def call(kernel, outs, ins, places=None, **more):
    return pl.pallas_call(
        kernel,
        out_shape=outs,
        in_specs=ins,
        out_specs=places or [VM] * len(outs),
        compiler_params=pltpu.CompilerParams(vmem_limit_bytes=LIMIT),
        **more,
    )


def iterate(
    plan, pay, right_side, jacobi_ids, needs, place, table, ends, ends_col, selfs, res, scale,
    freq, tables, couple_blocks,
):
    order, slots, rows = tables
    peers = needs.shape[0]
    devices = pay.shape[0]
    blocks, size, width = right_side.shape
    nodes = NODE_ROW * scale.shape[0] // PAD
    base = plan[0]
    far = [d for d in range(2, peers) if plan[d] > base]
    halo = kept((nodes + scale.shape[0] + (plan[1] - base) * size, width), bf16)
    vec = kept((blocks, size, width), f32)
    emitted = [
        vec,
        kept((peers, base, size, width), bf16),
        kept((CAP, size, width), bf16),
        halo,
        halo,
    ] + [kept((plan[d] - base, size, width), bf16) for d in far for side in range(2)]
    spots = [HB, HB] + [VM] * (len(emitted) - 2)
    buffers = [
        pltpu.VMEM((blocks, size, width), f32),
        pltpu.VMEM((blocks, size, width), bf16),
        pltpu.VMEM((peers, base, size, width), bf16),
        pltpu.VMEM((2 * nodes, width), bf16),
        pltpu.SemaphoreType.DMA((4,)),
    ]
    places = order.shape[1]
    coupling = [
        pltpu.VMEM((blocks, size, width), f32),
        pltpu.VMEM((peers * CAP + 2, size, width), bf16),
        pltpu.VMEM((places, size, size), bf16),
        pltpu.SemaphoreType.DMA((places // (RUN * QUAD),)),
    ]
    w, beta, z, send, own, right, left, *go = call(
        functools.partial(start_kernel, plan),
        [vec, whole((8, width), f32)] + emitted,
        [VM, VM, VM, SM, SM, SM, VM, VM],
        [HB, VM] + spots,
        scratch_shapes=[pltpu.VMEM((blocks, size, width), f32)] + buffers,
    )(near_core(pay), right_side, ends, jacobi_ids, needs, place, table, scale)
    basis = [w]
    fields = [z]
    for step in range(ITERS):

        def moved(value, distance):
            route = [(i, i + distance) for i in range(peers) if 0 <= i + distance < peers]
            return near_core(lax.ppermute(value, "narrow", route))

        arrived = moved(right, 1)
        beyond = moved(left, -1)
        come = []
        for at, d in enumerate(far):
            come += [moved(go[2 * at], d), moved(go[2 * at + 1], -d)]
        incoming = near_core(lax.all_to_all(send, "narrow", 0, 0))
        parts = 2 if blocks % 16 == 0 else 1
        block = pl.BlockSpec((blocks // parts, size, width), lambda i: (i, 0, 0))
        line = pl.BlockSpec((blocks // parts, size), lambda i: (i, 0))
        (part,) = call(
            local_kernel, [vec], [block, block, line, VM], [block], grid=(parts,)
        )(in_hbm(z), selfs, res, in_hbm(freq))
        head = pl.BlockSpec((nodes, width), lambda i: (0, 0))
        charge, plus = call(
            charge_kernel,
            [pltpu.VMEM((2 * nodes, width), bf16), pltpu.VMEM((16, 2 * nodes), bf16)],
            [VM, head, head, VM, VM],
            grid=(1,),
            cost_estimate=pl.CostEstimate(
                flops=WEIGHT * blocks * size * nodes * width,
                bytes_accessed=WEIGHT * blocks * size * width,
                transcendentals=0,
            ),
        )(scale, in_hbm(left), in_hbm(right), arrived, beyond)
        first = step == 0
        held = couple_blocks if first else sorted_blocks
        common = (
            rows, slots, place, in_hbm(held), incoming, in_hbm(own), arrived, beyond, *come,
            in_hbm(part), in_hbm(freq), ends_col, charge, plus,
        )
        specs = [SM, SM, SM, HB] + [VM] * (4 + len(come)) + [HB] + [VM] * 4
        if step + 1 < ITERS:
            w, z, send, own, right, left, *more = call(
                functools.partial(middle_kernel, plan, first),
                [vec] + emitted + ([kept((places, size, size), bf16)] if first else []),
                specs + [VM, SM, SM, VM, VM] + ([SM] if first else []),
                [HB] + spots + ([HB] if first else []),
                scratch_shapes=coupling + [pltpu.VMEM((blocks, size, width), f32)] + buffers,
            )(*common, ends, jacobi_ids, needs, table, scale, *([order] if first else []))
            go = more[: extras(plan)]
            if first:
                sorted_blocks = more[-1]
            basis.append(w)
            fields.append(z)
        else:
            (sums,) = call(
                functools.partial(last_kernel, plan),
                [whole((devices, 8, 128), f32)],
                specs + [HB] * 3,
                scratch_shapes=coupling
                + [
                    pltpu.VMEM((ITERS + 1, blocks, size, width), f32),
                    pltpu.SemaphoreType.DMA((ITERS + 1,)),
                ],
            )(*common, *map(in_hbm, basis))
    sums = near_core(lax.all_to_all(sums, AXES, 0, 0))
    parts = 4
    while blocks % parts:
        parts //= 2
    return call(
        finish_kernel,
        [vec, whole((CASES, F), f32)],
        [VM, VM] + [HB] * ITERS,
        [HB, VM],
        scratch_shapes=[
            pltpu.VMEM((ITERS, blocks, size, width), f32),
            pltpu.VMEM((blocks, size, width), f32),
            pltpu.SemaphoreType.DMA((parts, ITERS)),
            pltpu.SemaphoreType.DMA((parts,)),
        ],
    )(
        sums, beta, *map(in_hbm, fields)
    )


def on_device(
    right_side, resistance, omega, pcoef, branch_nodes, self_blocks, couple_list, couple_blocks,
    jacobi_ids, preconditioners,
):
    blocks, size, width = right_side.shape
    nodes = pcoef.shape[0]
    entries = couple_list.shape[1]
    peers = lax.axis_size("narrow")
    devices = peers * lax.axis_size("wide")
    group = lax.axis_index("wide")
    mine = lax.axis_index("narrow")
    node_rows = nodes // NODE_ROW
    pairs = jnp.transpose(branch_nodes, (1, 0, 2)).reshape(2, blocks * size)
    pairs = jnp.where(pairs[0] == pairs[1], -1, pairs)
    quads = (entries + (QUAD - 1) * blocks) // QUAD
    quads = -(-quads // RUN) * RUN

    (pay,) = call(
        functools.partial(setup_kernel, peers, blocks),
        [whole((devices, 8, 128), f32)],
        [VM] * 2,
    )(in_hbm(couple_list), in_hbm(right_side))
    pay = lax.all_to_all(pay, AXES, 0, 0)
    order, slots, rows, ends, rows16, ends_col, freq = call(
        functools.partial(order_kernel, peers, blocks),
        [
            whole((1, quads * QUAD), i32),
            whole((1, quads * QUAD), i32),
            whole((1, quads), i32),
            kept((32, blocks * size), i16),
            kept((PAD * node_rows, NODE_ROW), bf16),
            kept((blocks * size, 2), i16),
            kept((1, width), f32),
        ],
        [VM] * 4,
    )(couple_list, pairs, pcoef.reshape(node_rows, NODE_ROW), omega.reshape(1, -1))
    needs = lax.dynamic_slice(
        pay, (group * peers, 1, mine * CAP), (peers, 1, CAP)
    ).reshape(peers, CAP).astype(i32)
    shared = (
        pay, in_hbm(right_side), jacobi_ids, needs, mine.reshape(1), in_hbm(preconditioners),
        in_hbm(ends), in_hbm(ends_col), in_hbm(self_blocks),
        in_hbm(resistance), in_hbm(rows16), freq, (order, slots, rows),
        in_hbm(couple_blocks),
    )
    full = (CAP,) * peers
    near = (1,) + tuple(max(1, CAP // distance) for distance in range(1, peers))
    reach = np.abs(np.arange(devices)[:, None] % peers - np.arange(peers)[None, :])
    allowed = np.where(reach == 0, CAP, np.asarray(near)[reach]).astype(np.float32)
    fits = jnp.all(pay[:, 2, :peers] <= allowed)
    return lax.cond(
        fits, lambda given: iterate(near, *given), lambda given: iterate(full, *given), shared
    )


def solution(mesh):
    placed = (
        P(AXES, None, None),
        P(AXES, None),
        P(),
        P(AXES),
        P(AXES, None, None),
        P(AXES, None, None),
        P(None, AXES),
        P(AXES, None, None),
        P(AXES),
        P(),
    )
    return jax.shard_map(
        on_device,
        mesh=mesh,
        in_specs=placed,
        out_specs=(P(AXES, None, None), P()),
        check_vma=False,
    )
```

```python
import functools
import jax
import jax.numpy as jnp
import numpy as np
from jax import lax
from jax.experimental import pallas as pl
from jax.experimental.pallas import tpu as pltpu
from jax.sharding import PartitionSpec as P

F = 32
CASES = 2
ITERS = 3
CAP = 4
AXES = ("wide", "narrow")
STEP = 2.0**-8
LIMIT = 40 * 1024 * 1024
QUAD = 4
RUN = 17
WEIGHT = 64
NODE_ROW = 128
PAD = 2
f32 = jnp.float32
bf16 = jnp.bfloat16
i32 = jnp.int32
i16 = jnp.int16


def whole(shape, dtype):
    return jax.ShapeDtypeStruct(shape, dtype)


def kept(shape, dtype):
    return pltpu.HBM(shape, dtype)


def in_hbm(value):
    return pltpu.with_memory_space_constraint(value, pltpu.HBM)


def near_core(value):
    return pltpu.with_memory_space_constraint(value, pltpu.VMEM)


VM = pl.BlockSpec(memory_space=pltpu.VMEM)
SM = pl.BlockSpec(memory_space=pltpu.SMEM)
HB = pl.BlockSpec(memory_space=pl.ANY)


def lane_is_real(shape):
    lane = lax.broadcasted_iota(i32, shape, len(shape) - 1)
    return lax.rem(lane, 2 * F) < F


def both_parts(row):
    other = jnp.where(lane_is_real(row.shape), pltpu.roll(row, 128 - F, 1), pltpu.roll(row, F, 1))
    return row + other


def turned(values):
    return jnp.where(
        lane_is_real(values.shape),
        -pltpu.roll(values, 128 - F, 1),
        pltpu.roll(values, F, 1),
    )


def block_ranks(peers, blocks, lists_ref):
    keys = peers * blocks
    entries = lists_ref.shape[1]
    key = lists_ref[2:3, :] * blocks + lists_ref[1:2, :]
    one = (lax.broadcasted_iota(i32, (keys, entries), 0) == key).astype(f32)
    present = jnp.max(one, axis=1, keepdims=True)
    row = lax.broadcasted_iota(i32, (keys, keys), 0)
    col = lax.broadcasted_iota(i32, (keys, keys), 1)
    before = jnp.where((row // blocks == col // blocks) & (col <= row), 1.0, 0.0).astype(bf16)
    rank = jnp.dot(
        before,
        jnp.broadcast_to(present, (keys, 128)).astype(bf16),
        preferred_element_type=f32,
    )
    return one, present, rank


def setup_kernel(peers, blocks, lists_ref, right_ref, pay_ref):
    keys = peers * blocks
    _, present, rank = block_ranks(peers, blocks, lists_ref)
    lane = lax.broadcasted_iota(i32, (keys, 128), 1)
    name = lax.broadcasted_iota(i32, (keys, 128), 0)
    chosen = (
        (name // blocks == lane // CAP)
        & (rank == (lane % CAP + 1).astype(f32))
        & (present > 0.0)
    )
    needs = jnp.sum(jnp.where(chosen, (name % blocks).astype(f32), 0.0), axis=0, keepdims=True)
    held = jnp.sum(jnp.where(name // blocks == lane, present, 0.0), axis=0, keepdims=True)
    right = right_ref[...]
    squares = jnp.sum(jnp.sum(right * right, axis=0), axis=0, keepdims=True)
    rows = jnp.concatenate([squares, needs, held], axis=0)
    pay_ref[...] = jnp.broadcast_to(rows[None], pay_ref.shape)


def order_kernel(
    peers, blocks, lists_ref, pairs_ref, pcoef_ref, omega_ref, order_ref, slot_ref, row_ref, ends_ref,
    rows_ref, cols_ref, freq_ref,
):
    for k in range(2):
        row = jnp.broadcast_to(pairs_ref[k : k + 1, :], (16, pairs_ref.shape[1]))
        ends_ref[16 * k : 16 * (k + 1), :] = row.astype(i16)
    numbers = pairs_ref[...].astype(f32)
    numbers = jnp.concatenate([numbers, jnp.zeros((6, numbers.shape[1]), f32)], axis=0)
    cols_ref[...] = jnp.transpose(numbers)[:, :2].astype(i32).astype(i16)
    freq_ref[...] = jnp.concatenate([omega_ref[...]] * (2 * CASES), axis=1)
    own = pcoef_ref[...]
    rows_ref[...] = jnp.concatenate([own, jnp.zeros_like(own)], axis=0).astype(bf16)
    entries = lists_ref.shape[1]
    places = order_ref.shape[1]
    quads = row_ref.shape[1]
    one, _, rank = block_ranks(peers, blocks, lists_ref)
    place = jnp.sum(one * (rank[:, :1] - 1.0), axis=0, keepdims=True)
    slot = (lists_ref[2:3, :] * CAP).astype(f32) + place
    mine = (lax.broadcasted_iota(i32, (blocks, entries), 0) == lists_ref[0:1, :]).astype(f32)
    earlier = lax.broadcasted_iota(i32, (entries, entries), 0) < lax.broadcasted_iota(
        i32, (entries, entries), 1
    )
    seen = jnp.dot(
        mine.astype(bf16), jnp.where(earlier, 1.0, 0.0).astype(bf16), preferred_element_type=f32
    )
    turn = jnp.sum(mine * seen, axis=0, keepdims=True).astype(i32)
    count = jnp.sum(mine, axis=1, keepdims=True).astype(i32)
    groups = (count + QUAD - 1) // QUAD
    above = lax.broadcasted_iota(i32, (blocks, blocks), 1) < lax.broadcasted_iota(
        i32, (blocks, blocks), 0
    )
    base = jnp.dot(
        jnp.where(above, 1.0, 0.0).astype(bf16),
        jnp.broadcast_to(groups.astype(f32), (blocks, 128)).astype(bf16),
        preferred_element_type=f32,
    )[:, :1]
    start = jnp.sum(mine * base, axis=0, keepdims=True).astype(i32)
    goal = (start + turn // QUAD) * QUAD + turn % QUAD
    found = (lax.broadcasted_iota(i32, (places, entries), 0) == goal).astype(f32).astype(bf16)
    number = lax.broadcasted_iota(i32, (1, entries), 1).astype(f32)
    facts = jnp.concatenate(
        [number, slot, jnp.ones((1, entries), f32), jnp.zeros((5, entries), f32)], axis=0
    )
    table = lax.dot_general(
        facts.astype(bf16), found, (((1,), (1,)), ((), ())), preferred_element_type=f32
    )
    order_ref[...] = table[0:1, :].astype(i32)
    slot_ref[...] = jnp.where(table[2:3, :] > 0.5, table[1:2, :], float(peers * CAP)).astype(i32)
    quad = lax.broadcasted_iota(i32, (blocks, quads), 1).astype(f32)
    inside = (quad >= base) & (quad < base + groups.astype(f32))
    name = lax.broadcasted_iota(i32, (blocks, quads), 0)
    row_ref[...] = jnp.sum(jnp.where(inside, name.astype(f32), 0.0), axis=0, keepdims=True).astype(i32)


def signs(node, first, second):
    one = jnp.ones(node.shape, bf16)
    return jnp.where(node == first, one, jnp.where(node == second, -one, jnp.zeros_like(one)))


def charges(ends_ref, zb_ref, start, chunk):
    blocks, size, width = zb_ref.shape
    branches = blocks * size
    node = lax.broadcasted_iota(i32, (16, branches), 0).astype(i16)
    groups = []
    for g in range(chunk // 16):
        row = node + jnp.full((16, branches), start + 16 * g, i32).astype(i16)
        groups.append(signs(row, ends_ref[:16, :], ends_ref[16:, :]))
    return jnp.dot(
        jnp.concatenate(groups, axis=0),
        zb_ref[...].reshape(branches, width),
        preferred_element_type=f32,
    ).astype(bf16)


def emit(
    plan, w_of, ends_ref, jacobi_ref, needs_ref, place_ref, table_ref, rows_ref,
    z_ref, send_ref, own_ref, right_ref, left_ref, go_refs, zv_ref, zb_ref, sv_ref, both_ref, sems,
):
    blocks, size, width = zb_ref.shape
    peers = needs_ref.shape[0]
    base = plan[0]
    node_rows = rows_ref.shape[0]
    nodes = right_ref.shape[0] - (plan[1] - base) * size - node_rows
    for n in range(blocks):
        z = jnp.dot(table_ref[jacobi_ref[n]], w_of(n).astype(bf16), preferred_element_type=f32)
        zv_ref[n] = z
        zb_ref[n] = z.astype(bf16)
    for j in range(peers):
        for s in range(base):
            sv_ref[j, s] = zb_ref[needs_ref[j, s]]
    pack = pltpu.make_async_copy(sv_ref, send_ref, sems.at[1])
    pack.start()
    save = pltpu.make_async_copy(zv_ref, z_ref, sems.at[0])
    save.start()
    mine = place_ref[0]
    for s in range(CAP):
        own_ref[s] = zb_ref[needs_ref[mine, s]]
    left_ref[pl.ds(nodes, node_rows), :] = rows_ref[...]
    right_ref[pl.ds(nodes, node_rows), :] = rows_ref[...]
    for s in range(base, plan[1]):
        for out, step in ((right_ref, 1), (left_ref, -1)):
            peer = jnp.clip(mine + step, 0, peers - 1)
            there = nodes + node_rows + (s - base) * size
            out[pl.ds(there, size), :] = zb_ref[needs_ref[peer, s]]
    at = 0
    for distance in range(2, peers):
        if plan[distance] > base:
            for step in (distance, -distance):
                peer = jnp.clip(mine + step, 0, peers - 1)
                for s in range(base, plan[distance]):
                    go_refs[at][s - base] = zb_ref[needs_ref[peer, s]]
                at += 1
    chunk = nodes if base < CAP else 128

    def body(step, carry):
        start = pl.multiple_of(step * chunk, chunk)
        both_ref[pl.ds(start, chunk), :] = charges(ends_ref, zb_ref, start, chunk)
        return carry

    lax.fori_loop(0, 2 * nodes // chunk, body, 0)
    left_ref[pl.ds(0, nodes), :] = both_ref[pl.ds(0, nodes), :]
    right_ref[pl.ds(0, nodes), :] = both_ref[pl.ds(nodes, nodes), :]
    save.wait()
    pack.wait()


def start_kernel(
    plan, pay_ref, side_ref, ends_ref, jacobi_ref, needs_ref, place_ref, table_ref, rows_ref,
    w_ref, beta_ref, z_ref, send_ref, own_ref, right_ref, left_ref, *rest,
):
    go, rest = split(plan, rest)
    wv_ref, zv_ref, zb_ref, sv_ref, both_ref, sems = rest
    total = jnp.sum(pay_ref[:, 0, :], axis=0, keepdims=True)
    beta = jnp.sqrt(both_parts(total))
    beta_ref[...] = jnp.broadcast_to(beta, beta_ref.shape)
    wv_ref[...] = side_ref[...] / beta[None]
    save = pltpu.make_async_copy(wv_ref, w_ref, sems.at[2])
    save.start()
    emit(
        plan, lambda n: wv_ref[n], ends_ref, jacobi_ref, needs_ref, place_ref, table_ref, rows_ref,
        z_ref, send_ref, own_ref, right_ref, left_ref, go, zv_ref, zb_ref, sv_ref, both_ref, sems,
    )
    save.wait()


def local_kernel(z_ref, self_ref, res_ref, freq_ref, part_ref):
    freq = freq_ref[...]
    res = jnp.transpose(res_ref[...])
    for n in range(z_ref.shape[0]):
        z = z_ref[n]
        flux = jnp.dot(self_ref[n], z.astype(bf16), preferred_element_type=f32)
        part_ref[n] = freq * flux - turned(res[:, n : n + 1] * z)


def charge_kernel(rows_ref, left_ref, right_ref, arrived_ref, beyond_ref, charge_ref, plus_ref):
    node_rows = rows_ref.shape[0]
    nodes = NODE_ROW * node_rows // PAD
    charge_ref[:nodes] = (left_ref[...].astype(f32) + arrived_ref[:nodes].astype(f32)).astype(bf16)
    charge_ref[nodes:] = (right_ref[...].astype(f32) + beyond_ref[:nodes].astype(f32)).astype(bf16)
    own = rows_ref[...].astype(f32)
    next_rows = beyond_ref[pl.ds(nodes, node_rows), :].astype(f32)
    lanes = [own[i : i + 1, :] for i in range(nodes // NODE_ROW)]
    lanes += [next_rows[i : i + 1, :] for i in range(nodes // NODE_ROW)]
    row = jnp.concatenate(lanes, axis=1)
    plus_ref[...] = jnp.broadcast_to(row, (16, 2 * nodes)).astype(bf16)


def drop_into(acc_ref, group, beside, freq_ref, cols_ref, charge_ref, plus_ref):
    blocks, size, width = acc_ref.shape
    scale = 1.0 / (freq_ref[...] * freq_ref[...])

    def body(step, carry):
        start = pl.multiple_of(step * group * size, group * size)
        beside(step)
        plus = plus_ref[...]
        node = lax.broadcasted_iota(i32, plus.shape, 1).astype(i16)
        none = jnp.zeros_like(plus)
        rows = []
        for g in range(group * size // 16):
            ends = cols_ref[pl.ds(start + 16 * g, 16), :]
            rows.append(
                jnp.where(node == ends[:, 0:1], plus, jnp.where(node == ends[:, 1:2], -plus, none))
            )
        drop = jnp.dot(jnp.concatenate(rows, axis=0), charge_ref[...], preferred_element_type=f32)
        acc_ref[pl.ds(step * group, group)] = -(drop * scale).reshape(group, size, width)
        return carry

    lax.fori_loop(0, blocks // group, body, 0)


def couple(
    plan, order_ref, row_ref, slot_ref, place_ref, blocks_ref, incoming_ref, own_ref, arrived_ref,
    beyond_ref, extra_refs, drop_refs, acc_ref, source_ref, held_ref, sems, later,
):
    places = held_ref.shape[0]
    piece = RUN * QUAD
    runs = places // piece

    def copy(step):
        here = pl.ds(step * piece, piece)
        source = held_ref if order_ref is not None else blocks_ref
        return pltpu.make_async_copy(source.at[here], held_ref.at[here], sems.at[step])

    def fetch(i, carry, step):
        p = step * piece + i
        pltpu.make_async_copy(
            blocks_ref.at[order_ref[0, p]], held_ref.at[p], sems.at[step]
        ).start()
        return carry

    if order_ref is None:
        for step in range(runs):
            copy(step).start()
    for fetched in later:
        fetched.start()
    peers, base, size, width = incoming_ref.shape
    extra = plan[1] - base
    head = arrived_ref.shape[0] - extra * size
    mine = place_ref[0]
    for j in range(peers):
        for s in range(base):
            source_ref[j * CAP + s] = incoming_ref[j, s]
    source_ref[peers * CAP] = jnp.zeros((size, width), bf16)
    for s in range(base, CAP):
        source_ref[mine * CAP + s] = own_ref[s]
    for distance in range(1, peers):
        for s in range(base, plan[distance]):
            for side in range(2):
                peer = mine + (-distance if side == 0 else distance)
                there = (peer >= 0) & (peer < peers)
                slot = jnp.where(there, peer * CAP + s, peers * CAP + 1)
                if distance == 1:
                    source = arrived_ref if side == 0 else beyond_ref
                    block = source[pl.ds(head + (s - base) * size, size), :]
                else:
                    block = extra_refs[2 * (distance - 2) + side][s - base]
                source_ref[slot] = block
    halves = base < CAP and runs % 2 == 0

    def beside(step):
        if order_ref is not None and halves:
            for r in range(runs // 2):
                for i in range(piece):
                    fetch(i, 0, step=step * (runs // 2) + r)

    if order_ref is not None and not halves:
        for step in range(runs):
            lax.fori_loop(0, piece, functools.partial(fetch, step=step), 0)
    drop_into(acc_ref, acc_ref.shape[0] // 2 if base < CAP else 1, beside, *drop_refs)

    def body(step, carry):
        copy(step).wait()
        for u in range(RUN):
            quad = step * RUN + u
            left = jnp.concatenate([held_ref[quad * QUAD + i] for i in range(QUAD)], axis=1)
            right = jnp.concatenate(
                [source_ref[slot_ref[0, quad * QUAD + i]] for i in range(QUAD)], axis=0
            )
            acc_ref[row_ref[0, quad]] += jnp.dot(left, right, preferred_element_type=f32)
        return carry

    lax.fori_loop(0, runs, body, 0)
    for fetched in later:
        fetched.wait()


def image_of(part_ref, freq_ref, acc_ref, n):
    return STEP * turned(part_ref[n] + freq_ref[...] * acc_ref[n])


def split(plan, rest):
    count = extras(plan)
    return rest[:count], rest[count:]


def extras(plan):
    return 2 * sum(1 for slots in plan[2:] if slots > plan[0])


def middle_kernel(
    plan, first, row_ref, slot_ref, place_ref, blocks_ref, incoming_ref, own_in_ref, arrived_ref,
    beyond_ref, *rest,
):
    come, rest = split(plan, rest)
    part_ref, freq_ref, cols_ref, charge_ref, plus_ref = rest[:5]
    ends_ref, jacobi_ref, needs_ref, table_ref, rows_ref = rest[5:10]
    rest = rest[10:]
    order_ref = None
    if first:
        order_ref, rest = rest[0], rest[1:]
    w_ref, z_ref, send_ref, own_ref, right_ref, left_ref = rest[:6]
    go, rest = split(plan, rest[6:])
    if first:
        sorted_ref, rest = rest[0], rest[1:]
    acc_ref, source_ref, held_ref, run_sems, wv_ref, zv_ref, zb_ref, sv_ref, both_ref, sems = rest
    bring = pltpu.make_async_copy(part_ref, zv_ref, sems.at[0])
    couple(
        plan, order_ref, row_ref, slot_ref, place_ref, blocks_ref, incoming_ref, own_in_ref,
        arrived_ref, beyond_ref, come, (freq_ref, cols_ref, charge_ref, plus_ref), acc_ref,
        source_ref, held_ref, run_sems, [bring],
    )
    if first:
        keep = pltpu.make_async_copy(held_ref, sorted_ref, sems.at[3])
        keep.start()
    for n in range(wv_ref.shape[0]):
        wv_ref[n] = image_of(zv_ref, freq_ref, acc_ref, n)
    save = pltpu.make_async_copy(wv_ref, w_ref, sems.at[2])
    save.start()
    emit(
        plan, lambda n: wv_ref[n], ends_ref, jacobi_ref, needs_ref, place_ref, table_ref, rows_ref,
        z_ref, send_ref, own_ref, right_ref, left_ref, go, zv_ref, zb_ref, sv_ref, both_ref, sems,
    )
    save.wait()
    if first:
        keep.wait()


PAIRS = [(i, j) for j in range(ITERS + 1) for i in range(j + 1)]


def last_kernel(
    plan, row_ref, slot_ref, place_ref, blocks_ref, incoming_ref, own_ref, arrived_ref,
    beyond_ref, *rest,
):
    come, rest = split(plan, rest)
    part_ref, freq_ref, cols_ref, charge_ref, plus_ref = rest[:5]
    w0_ref, w1_ref, w2_ref, pay_ref = rest[5:9]
    acc_ref, source_ref, held_ref, run_sems, store_ref, sems = rest[9:]
    bring = [
        pltpu.make_async_copy(source, store_ref.at[at], sems.at[at])
        for at, source in enumerate((part_ref, w0_ref, w1_ref, w2_ref))
    ]
    couple(
        plan, None, row_ref, slot_ref, place_ref, blocks_ref, incoming_ref, own_ref,
        arrived_ref, beyond_ref, come, (freq_ref, cols_ref, charge_ref, plus_ref), acc_ref,
        source_ref, held_ref, run_sems, bring,
    )
    blocks = acc_ref.shape[0]

    def body(n, sums):
        w = [store_ref[1 + k, n] for k in range(ITERS)]
        w.append(image_of(store_ref.at[0], freq_ref, acc_ref, n))
        fresh = []
        for at, (i, j) in enumerate(PAIRS):
            product = (w[i] * w[j]).reshape(-1, 8, 128)
            fresh.append(sums[at] + jnp.sum(product, axis=0))
        return tuple(fresh)

    sums = lax.fori_loop(0, blocks, body, tuple(jnp.zeros((8, 128), f32) for _ in PAIRS))
    rows = [jnp.sum(s, axis=0, keepdims=True) for s in sums]
    rows = [both_parts(row) for row in rows]
    real = lane_is_real((1, 128))
    rows = [jnp.where(real, rows[k], rows[k + 1]) for k in range(0, len(rows), 2)]
    rows.append(jnp.zeros((8 - len(rows), 128), f32))
    pay_ref[...] = jnp.broadcast_to(jnp.concatenate(rows, axis=0)[None], pay_ref.shape)


def finish_kernel(
    pay_ref, beta_ref, z0_ref, z1_ref, z2_ref, out_ref, norm_ref, held_ref, made_ref, in_sems, out_sems,
):
    parts = out_sems.shape[0]
    group = out_ref.shape[0] // parts
    arrive = []
    for p in range(parts):
        here = pl.ds(p * group, group)
        arrive.append(
            [
                pltpu.make_async_copy(z.at[here], held_ref.at[k, here], in_sems.at[p, k])
                for k, z in enumerate((z0_ref, z1_ref, z2_ref))
            ]
        )
        for copy in arrive[p]:
            copy.start()
    total = jnp.sum(pay_ref[...], axis=0)
    real = lane_is_real(total.shape)
    even = jnp.where(real, total, pltpu.roll(total, F, 1))
    odd = jnp.where(real, pltpu.roll(total, 128 - F, 1), total)
    gram = {}
    for at, (i, j) in enumerate(PAIRS):
        half = at // 2
        gram[i, j] = gram[j, i] = (odd if at % 2 else even)[half : half + 1, :]
    order = list(range(1, ITERS + 1)) + [0]
    low = {}
    for i in range(ITERS + 1):
        for j in range(i + 1):
            value = gram[order[i], order[j]]
            for k in range(j):
                value = value - low[i, k] * low[j, k]
            low[i, j] = jnp.sqrt(jnp.maximum(value, 0.0)) if i == j else value / low[j, j]
    weights = [None] * ITERS
    for i in reversed(range(ITERS)):
        value = low[ITERS, i]
        for k in range(i + 1, ITERS):
            value = value - low[k, i] * weights[k]
        weights[i] = value / low[i, i]
    beta = beta_ref[0:1, :]
    norm = low[ITERS, ITERS] * beta
    norm_ref[...] = jnp.concatenate([norm, pltpu.roll(norm, 2 * F, 1)], axis=0)[:, :F]
    weights = [STEP * beta * weight for weight in weights]
    leave = []
    for p in range(parts):
        for copy in arrive[p]:
            copy.wait()
        for n in range(p * group, (p + 1) * group):
            total = weights[0] * held_ref[0, n]
            for k in range(1, ITERS):
                total = total + weights[k] * held_ref[k, n]
            made_ref[n] = total
        here = pl.ds(p * group, group)
        leave.append(pltpu.make_async_copy(made_ref.at[here], out_ref.at[here], out_sems.at[p]))
        leave[p].start()
    for copy in leave:
        copy.wait()


def call(kernel, outs, ins, places=None, **more):
    return pl.pallas_call(
        kernel,
        out_shape=outs,
        in_specs=ins,
        out_specs=places or [VM] * len(outs),
        compiler_params=pltpu.CompilerParams(vmem_limit_bytes=LIMIT),
        **more,
    )


def iterate(
    plan, pay, right_side, jacobi_ids, needs, place, table, ends, ends_col, selfs, res, scale,
    freq, tables, couple_blocks,
):
    order, slots, rows = tables
    peers = needs.shape[0]
    devices = pay.shape[0]
    blocks, size, width = right_side.shape
    nodes = NODE_ROW * scale.shape[0] // PAD
    base = plan[0]
    far = [d for d in range(2, peers) if plan[d] > base]
    halo = kept((nodes + scale.shape[0] + (plan[1] - base) * size, width), bf16)
    vec = kept((blocks, size, width), f32)
    emitted = [
        vec,
        kept((peers, base, size, width), bf16),
        kept((CAP, size, width), bf16),
        halo,
        halo,
    ] + [kept((plan[d] - base, size, width), bf16) for d in far for side in range(2)]
    spots = [HB, HB] + [VM] * (len(emitted) - 2)
    buffers = [
        pltpu.VMEM((blocks, size, width), f32),
        pltpu.VMEM((blocks, size, width), bf16),
        pltpu.VMEM((peers, base, size, width), bf16),
        pltpu.VMEM((2 * nodes, width), bf16),
        pltpu.SemaphoreType.DMA((4,)),
    ]
    places = order.shape[1]
    coupling = [
        pltpu.VMEM((blocks, size, width), f32),
        pltpu.VMEM((peers * CAP + 2, size, width), bf16),
        pltpu.VMEM((places, size, size), bf16),
        pltpu.SemaphoreType.DMA((places // (RUN * QUAD),)),
    ]
    w, beta, z, send, own, right, left, *go = call(
        functools.partial(start_kernel, plan),
        [vec, whole((8, width), f32)] + emitted,
        [VM, VM, VM, SM, SM, SM, VM, VM],
        [HB, VM] + spots,
        scratch_shapes=[pltpu.VMEM((blocks, size, width), f32)] + buffers,
    )(near_core(pay), right_side, ends, jacobi_ids, needs, place, table, scale)
    basis = [w]
    fields = [z]
    for step in range(ITERS):

        def moved(value, distance):
            route = [(i, i + distance) for i in range(peers) if 0 <= i + distance < peers]
            return near_core(lax.ppermute(value, "narrow", route))

        arrived = moved(right, 1)
        beyond = moved(left, -1)
        come = []
        for at, d in enumerate(far):
            come += [moved(go[2 * at], d), moved(go[2 * at + 1], -d)]
        incoming = near_core(lax.all_to_all(send, "narrow", 0, 0))
        parts = 2 if blocks % 16 == 0 else 1
        block = pl.BlockSpec((blocks // parts, size, width), lambda i: (i, 0, 0))
        line = pl.BlockSpec((blocks // parts, size), lambda i: (i, 0))
        (part,) = call(
            local_kernel, [vec], [block, block, line, VM], [block], grid=(parts,)
        )(in_hbm(z), selfs, res, in_hbm(freq))
        head = pl.BlockSpec((nodes, width), lambda i: (0, 0))
        charge, plus = call(
            charge_kernel,
            [pltpu.VMEM((2 * nodes, width), bf16), pltpu.VMEM((16, 2 * nodes), bf16)],
            [VM, head, head, VM, VM],
            grid=(1,),
            cost_estimate=pl.CostEstimate(
                flops=WEIGHT * blocks * size * nodes * width,
                bytes_accessed=WEIGHT * blocks * size * width,
                transcendentals=0,
            ),
        )(scale, in_hbm(left), in_hbm(right), arrived, beyond)
        first = step == 0
        held = couple_blocks if first else sorted_blocks
        common = (
            rows, slots, place, in_hbm(held), incoming, in_hbm(own), arrived, beyond, *come,
            in_hbm(part), in_hbm(freq), ends_col, charge, plus,
        )
        specs = [SM, SM, SM, HB] + [VM] * (4 + len(come)) + [HB] + [VM] * 4
        if step + 1 < ITERS:
            w, z, send, own, right, left, *more = call(
                functools.partial(middle_kernel, plan, first),
                [vec] + emitted + ([kept((places, size, size), bf16)] if first else []),
                specs + [VM, SM, SM, VM, VM] + ([SM] if first else []),
                [HB] + spots + ([HB] if first else []),
                scratch_shapes=coupling + [pltpu.VMEM((blocks, size, width), f32)] + buffers,
            )(*common, ends, jacobi_ids, needs, table, scale, *([order] if first else []))
            go = more[: extras(plan)]
            if first:
                sorted_blocks = more[-1]
            basis.append(w)
            fields.append(z)
        else:
            (sums,) = call(
                functools.partial(last_kernel, plan),
                [whole((devices, 8, 128), f32)],
                specs + [HB] * 3,
                scratch_shapes=coupling
                + [
                    pltpu.VMEM((ITERS + 1, blocks, size, width), f32),
                    pltpu.SemaphoreType.DMA((ITERS + 1,)),
                ],
            )(*common, *map(in_hbm, basis))
    sums = near_core(lax.all_to_all(sums, AXES, 0, 0))
    parts = 4
    while blocks % parts:
        parts //= 2
    return call(
        finish_kernel,
        [vec, whole((CASES, F), f32)],
        [VM, VM] + [HB] * ITERS,
        [HB, VM],
        scratch_shapes=[
            pltpu.VMEM((ITERS, blocks, size, width), f32),
            pltpu.VMEM((blocks, size, width), f32),
            pltpu.SemaphoreType.DMA((parts, ITERS)),
            pltpu.SemaphoreType.DMA((parts,)),
        ],
    )(
        sums, beta, *map(in_hbm, fields)
    )


def on_device(
    right_side, resistance, omega, pcoef, branch_nodes, self_blocks, couple_list, couple_blocks,
    jacobi_ids, preconditioners,
):
    blocks, size, width = right_side.shape
    nodes = pcoef.shape[0]
    entries = couple_list.shape[1]
    peers = lax.axis_size("narrow")
    devices = peers * lax.axis_size("wide")
    group = lax.axis_index("wide")
    mine = lax.axis_index("narrow")
    node_rows = nodes // NODE_ROW
    pairs = jnp.transpose(branch_nodes, (1, 0, 2)).reshape(2, blocks * size)
    pairs = jnp.where(pairs[0] == pairs[1], -1, pairs)
    quads = (entries + (QUAD - 1) * blocks) // QUAD
    quads = -(-quads // RUN) * RUN

    (pay,) = call(
        functools.partial(setup_kernel, peers, blocks),
        [whole((devices, 3, 128), f32)],
        [VM] * 2,
    )(in_hbm(couple_list), in_hbm(right_side))
    pay = lax.all_to_all(pay, AXES, 0, 0)
    order, slots, rows, ends, rows16, ends_col, freq = call(
        functools.partial(order_kernel, peers, blocks),
        [
            whole((1, quads * QUAD), i32),
            whole((1, quads * QUAD), i32),
            whole((1, quads), i32),
            kept((32, blocks * size), i16),
            kept((PAD * node_rows, NODE_ROW), bf16),
            kept((blocks * size, 2), i16),
            kept((1, width), f32),
        ],
        [VM] * 4,
    )(couple_list, pairs, pcoef.reshape(node_rows, NODE_ROW), omega.reshape(1, -1))
    needs = lax.dynamic_slice(
        pay, (group * peers, 1, mine * CAP), (peers, 1, CAP)
    ).reshape(peers, CAP).astype(i32)
    shared = (
        pay, in_hbm(right_side), jacobi_ids, needs, mine.reshape(1), in_hbm(preconditioners),
        in_hbm(ends), in_hbm(ends_col), in_hbm(self_blocks),
        in_hbm(resistance), in_hbm(rows16), freq, (order, slots, rows),
        in_hbm(couple_blocks),
    )
    full = (CAP,) * peers
    near = (1,) + tuple(max(1, CAP // distance) for distance in range(1, peers))
    reach = np.abs(np.arange(devices)[:, None] % peers - np.arange(peers)[None, :])
    allowed = np.where(reach == 0, CAP, np.asarray(near)[reach]).astype(np.float32)
    fits = jnp.all(pay[:, 2, :peers] <= allowed)
    return lax.cond(
        fits, lambda given: iterate(near, *given), lambda given: iterate(full, *given), shared
    )


def solution(mesh):
    placed = (
        P(AXES, None, None),
        P(AXES, None),
        P(),
        P(AXES),
        P(AXES, None, None),
        P(AXES, None, None),
        P(None, AXES),
        P(AXES, None, None),
        P(AXES),
        P(),
    )
    return jax.shard_map(
        on_device,
        mesh=mesh,
        in_specs=placed,
        out_specs=(P(AXES, None, None), P()),
        check_vma=False,
    )
```
